128 devices in a mesh: gx: 4 (over z), gy: 4 (over x), gz: 8 (over y, core).
Axes of the slice: x: 4, y: 4, z: 4, core: 2. Of those that a mesh axis runs over, the one named last changes fastest.
Arguments:
- orbitals: float32 [16, 128, 64, 512], P(None, 'gz', 'gy', 'gx'), may hold values from -12 to 12
- potential: float32 [128, 64, 512], P('gz', 'gy', 'gx'), may hold values from -4 to 4
Outputs:
- orthonormal: float32 [16, 128, 64, 512], P(None, 'gz', 'gy', 'gx')
- factor: float32 [16, 16], replicated
The draws below stay inside these ranges and needn't reach their ends.
All inputs are finite; a program needn't handle non-finite values.
Results may differ from the reference program's by a relative error of at most 0.00016.
Values sent between devices are 32-bit elements; how exact they have to be, the bound alone decides.
A program may use at most 192 MiB of HBM per device.

```python
import jax
import jax.numpy as jnp
from jax import lax

NORB = 16
NX = 512
NY = 64
NZ = 128
NCELLS = 4194304


def draw_orbitals(key, part):
    key = jax.random.fold_in(key, 7)
    shape = (NORB, NZ, NY, NX)
    place = jnp.arange(NX, dtype=jnp.float32) / NX
    values = jax.random.truncated_normal(key, -6.0, 6.0, shape, jnp.float32)
    envelope = 0.5 + 1.5 * place
    return values * envelope


def level_of(own_key, dims, cuts, least, top_value):
    def one(position, blocks):
        draws = jax.random.uniform(jax.random.fold_in(jax.random.fold_in(own_key, 6), position), (blocks,), jnp.float32, least / len(cuts), top_value / len(cuts))
        return jnp.repeat(jnp.exp(draws), dims[position] // blocks).reshape((-1,) + (1,) * (len(dims) - position - 1))

    loudness = one(*cuts[0])
    for cut in cuts[1:]:
        loudness = loudness * one(*cut)
    return loudness


def setup_inputs(seed: int = 0) -> dict:
    key_list = jax.random.split(jax.random.key(seed), 3)
    orbitals = draw_orbitals(jax.random.fold_in(key_list[2], 71), 0)
    potential = jnp.clip(jax.random.uniform(key_list[1], (NZ, NY, NX), jnp.float32, -4.0, 4.0) * level_of(key_list[1], (NZ, NY, NX), ((0, 8), (1, 4), (2, 4)), -0.4, 0.0), -4.0, 4.0)
    return dict(orbitals=orbitals, potential=potential)


COEFFS = (-205.0 / 72.0, 8.0 / 5.0, -1.0 / 5.0, 8.0 / 315.0, -1.0 / 560.0)
KINETIC = -2.0
CENTRE = 23.0
HALF_WIDTH = 20.0

def hamilton_ref(field, potential):
    total = 3.0 * COEFFS[0] * field
    for axis_pos in (0, 1, 2):
        for offset in range(1, 5):
            total = total + COEFFS[offset] * (jnp.roll(field, -offset, axis_pos) + jnp.roll(field, offset, axis_pos))
    return KINETIC * total + potential * field

def filter_one(field, potential):
    level_one = (hamilton_ref(field, potential) - CENTRE * field) / HALF_WIDTH
    level_two = 2.0 * (hamilton_ref(level_one, potential) - CENTRE * level_one) / HALF_WIDTH - field
    return 2.0 * (hamilton_ref(level_two, potential) - CENTRE * level_two) / HALF_WIDTH - level_one

def reference(orbitals, potential):
    filtered = lax.map(lambda field: filter_one(field, potential), orbitals)
    flat = filtered.reshape(filtered.shape[0], -1)
    gram = jnp.einsum('ac,bc->ab', flat, flat, precision=lax.Precision.HIGHEST) / jnp.float32(NCELLS)
    lower = jnp.linalg.cholesky(gram)
    solved = lax.linalg.triangular_solve(lower, flat, left_side=True, lower=True)
    return (solved.reshape(filtered.shape), lower.T)
```

```python
import functools

import jax
import jax.numpy as jnp
import ml_dtypes
import numpy as np
from jax import lax
from jax.experimental import pallas as pl
from jax.experimental.pallas import tpu as pltpu
from jax.sharding import PartitionSpec as P

COEFFS = (-205.0 / 72.0, 8.0 / 5.0, -1.0 / 5.0, 8.0 / 315.0, -1.0 / 560.0)
SCALE = 2.0 * -2.0 / 20.0
TAPS = tuple(SCALE * c for c in COEFFS)

NORB, LZ, LY, LX = 16, 16, 16, 128
HALO = 4
SUB = 8
GROUPS = NORB // SUB
SLABS = 4
CHUNKS = LZ // SLABS
UNITS = GROUPS * CHUNKS
ROWS = LZ * LY
CELLS = 4194304
F32, BF16 = jnp.float32, jnp.bfloat16
MESH = pl.DeviceIdType.MESH
AXES = ("gx", "gy", "gz")


def x_weights():
    places = np.concatenate([np.arange(LX), np.arange(-HALO, 0), np.arange(LX, LX + HALO)])
    away = np.abs(places[:, None] - np.arange(LX)[None, :])
    full = np.zeros((2 * LX, LX), np.float32)
    for k in range(1, HALO + 1):
        full[: len(places)][away == k] = np.float32(TAPS[k])
    high = full.astype(ml_dtypes.bfloat16)
    low = (full - high.astype(np.float32)).astype(ml_dtypes.bfloat16)
    return np.concatenate([high, low], axis=1)


def split(value):
    high = value.astype(BF16)
    return high, (value - high.astype(F32)).astype(BF16)


def filter_kernel(
    orb_hbm, pot_hbm, w_hbm, last, gram_ref,
    load, buf, pack, from_left, from_right, pv, w_ref, part, seen_xy, seen_z,
    load_sem, small_sem, ysend, yrecv, xsend, xrecv, zsend, zrecv, gsend, grecv,
):
    sizes = {axis: lax.axis_size(axis) for axis in AXES}
    here = {axis: lax.axis_index(axis) for axis in AXES}

    def at(axis, step):
        return {axis: lax.rem(here[axis] + (step + sizes[axis]), sizes[axis])}

    def load_copy(g, c):
        part = (pl.ds(g * SUB, SUB), pl.ds(c * SLABS * LY, SLABS * LY))
        return pltpu.make_async_copy(
            orb_hbm.at[part], load.at[part], load_sem.at[g * CHUNKS + c]
        )

    small = [
        pltpu.make_async_copy(pot_hbm, pv, small_sem.at[0]),
        pltpu.make_async_copy(w_hbm, w_ref, small_sem.at[1]),
    ]
    for g in range(GROUPS):
        for c in range(CHUNKS):
            load_copy(g, c).start()
    for copy in small:
        copy.start()

    def in_plane(k):
        other = lax.rem(here["gx"] * sizes["gy"] + here["gy"] + k, sizes["gx"] * sizes["gy"])
        return {"gx": other // sizes["gy"], "gy": lax.rem(other, sizes["gy"])}

    def in_column(k):
        return at("gz", k)

    others = [in_plane(k) for k in range(1, sizes["gx"] * sizes["gy"])]
    others += [in_column(k) for k in range(1, sizes["gz"])]
    barrier = pltpu.get_barrier_semaphore()
    for device in others:
        pl.semaphore_signal(barrier, inc=1, device_id=device, device_id_type=MESH)

    def remote(src, dst, send_sem, recv_sem, axis, step):
        return pltpu.make_async_remote_copy(
            src_ref=src, dst_ref=dst, send_sem=send_sem, recv_sem=recv_sem,
            device_id=at(axis, step), device_id_type=MESH,
        )

    def y_copies(level, g, c):
        u, zs = g * CHUNKS + c, pl.ds(HALO + c * SLABS, SLABS)
        level_buf = buf.at[level, g, zs]
        return [
            remote(
                level_buf.at[:, pl.ds(LY, HALO)], level_buf.at[:, pl.ds(0, HALO)],
                ysend.at[level, u, 0], yrecv.at[level, u, 0], "gy", 1,
            ),
            remote(
                level_buf.at[:, pl.ds(HALO, HALO)], level_buf.at[:, pl.ds(HALO + LY, HALO)],
                ysend.at[level, u, 1], yrecv.at[level, u, 1], "gy", -1,
            ),
        ]

    def x_copies(level, g, c):
        u, zs = g * CHUNKS + c, pl.ds(c * SLABS, SLABS)
        return [
            remote(
                pack.at[level, g, zs], from_left.at[level, g, zs],
                xsend.at[level, u, 0], xrecv.at[level, u, 0], "gx", 1,
            ),
            remote(
                pack.at[level, g, zs], from_right.at[level, g, zs],
                xsend.at[level, u, 1], xrecv.at[level, u, 1], "gx", -1,
            ),
        ]

    def z_copy(level, g, up):
        inner = pl.ds(HALO, LY)
        src, dst = (LZ, 0) if up else (HALO, HALO + LZ)
        i = 0 if up else 1
        return remote(
            buf.at[level, g, pl.ds(src, HALO), inner], buf.at[level, g, pl.ds(dst, HALO), inner],
            zsend.at[level, g, i], zrecv.at[level, g, i], "gz", 1 if up else -1,
        )

    def send(level, g, c):
        for copy in y_copies(level, g, c):
            copy.start()

        @pl.when(c == 0)
        def _():
            z_copy(level, g, False).start()

        @pl.when(c == CHUNKS - 1)
        def _():
            z_copy(level, g, True).start()

        for copy in x_copies(level, g, c):
            copy.start()

    lane = lax.broadcasted_iota(jnp.int32, (SUB, LX), 1)

    def pack_edges(values):
        packed = jnp.zeros((SUB, LX), F32)
        for y in range(LY):
            moved = pltpu.roll(values[y], 2 * HALO * y + HALO, 1)
            mine = (lane >= 2 * HALO * y) & (lane < 2 * HALO * (y + 1))
            packed = jnp.where(mine, moved, packed)
        return packed

    flat = load.reshape(NORB * ROWS, LX)

    def start_unit(g, c):
        load_copy(g, c).wait()

        @pl.loop(0, SLABS)
        def _(s):
            z = c * SLABS + s
            values = []
            for y in range(LY):
                v = flat[pl.ds(g * SUB * ROWS + z * LY + y, SUB, stride=ROWS), :]
                buf[0, g, HALO + z, HALO + y] = v
                values.append(v)
            pack[0, g, z] = pack_edges(values)

    start_unit(0, 0)
    pl.semaphore_wait(barrier, len(others))
    send(0, 0, 0)

    @pl.loop(1, UNITS)
    def _(u):
        g, c = u // CHUNKS, lax.rem(u, CHUNKS)
        start_unit(g, c)
        send(0, g, c)

    for copy in small:
        copy.wait()
    pv[...] = pv[...] * F32(0.1) + F32(3.0 * TAPS[0] - 2.3)

    def stencil(level, g, z):
        w = w_ref[...]
        edges = jnp.where(
            lax.rem(lane, 2 * HALO) < HALO, from_left[level, g, z], from_right[level, g, z]
        )
        centre = [buf[level, g, HALO + z, HALO + y] for y in range(LY)]
        rows = jnp.concatenate(centre, axis=0)
        halo = jnp.concatenate(
            [pltpu.roll(edges, (LX - 2 * HALO * y) % LX, 1) for y in range(LY)], axis=0
        )
        high, low = split(jnp.concatenate([rows, halo], axis=1))
        both = jnp.dot(high, w, preferred_element_type=F32)
        along_x = (
            jnp.dot(low, w[:, :LX], preferred_element_type=F32) + both[:, :LX] + both[:, LX:]
        )
        out = []
        for y in range(LY):
            here_v = centre[y]
            total = pv[z, pl.ds(y, 1), :] * here_v + along_x[y * SUB : (y + 1) * SUB]
            for k in range(1, HALO + 1):
                around = (
                    buf[level, g, HALO + z + k, HALO + y] + buf[level, g, HALO + z - k, HALO + y]
                ) + (buf[level, g, HALO + z, HALO + y + k] + buf[level, g, HALO + z, HALO + y - k])
                total = total + F32(TAPS[k]) * around
            out.append(total)
        return out

    def wait_halos(level, g, c):
        for copy in y_copies(level, g, c) + x_copies(level, g, c):
            copy.wait_recv()

        @pl.when(c == 0)
        def _():
            z_copy(level, g, True).wait_recv()

        @pl.when(c == CHUNKS - 1)
        def _():
            z_copy(level, g, False).wait_recv()

    for level in (1, 2):

        @pl.loop(0, UNITS)
        def _(u, level=level):
            g, c = u // CHUNKS, lax.rem(u, CHUNKS)
            wait_halos(level - 1, g, c)

            @pl.loop(0, SLABS)
            def _(s):
                z = c * SLABS + s
                new = stencil(level - 1, g, z)
                if level == 1:
                    new = [F32(0.5) * v for v in new]
                else:
                    new = [v - buf[0, g, HALO + z, HALO + y] for y, v in enumerate(new)]
                for y in range(LY):
                    buf[level, g, HALO + z, HALO + y] = new[y]
                pack[level, g, z] = pack_edges(new)

            send(level, g, c)

    part[...] = jnp.zeros_like(part)

    @pl.loop(0, UNITS)
    def _(u):
        g, c = u // CHUNKS, lax.rem(u, CHUNKS)
        wait_halos(2, g, c)

        @pl.loop(0, SLABS)
        def _(s):
            z = c * SLABS + s
            new = stencil(2, g, z)
            for y in range(LY):
                last[g, z, y] = new[y] - buf[1, g, HALO + z, HALO + y]

        @pl.when(g == GROUPS - 1)
        def _():
            @pl.loop(0, SLABS)
            def _(s):
                z = c * SLABS + s
                wide = jnp.concatenate(
                    [
                        jnp.concatenate([last[k, z, y] for k in range(GROUPS)], axis=0)
                        for y in range(LY)
                    ],
                    axis=1,
                )
                high, low = split(wide)
                both = jnp.concatenate([high, low], axis=0)
                quad = lax.dot_general(
                    both, both, (((1,), (1,)), ((), ())), preferred_element_type=F32
                )
                four = quad[:NORB] + quad[NORB:]
                part[:, :NORB] += four[:, :NORB] + four[:, NORB:]

    gram_copies = []
    moved = pltpu.roll(part[...] * F32(1.0 / CELLS), 0, 1, stride=NORB, stride_axis=0)
    value = jnp.sum(moved.reshape(2, SUB, LX), axis=1)
    plane = sizes["gx"] * sizes["gy"]
    base = 0
    for seen, count, mine, target in (
        (seen_xy, plane, here["gx"] * sizes["gy"] + here["gy"], in_plane),
        (seen_z, sizes["gz"], here["gz"], in_column),
    ):
        seen[mine] = value
        copies = []
        for k in range(1, count):
            copies.append(
                pltpu.make_async_remote_copy(
                    src_ref=seen.at[mine], dst_ref=seen.at[mine], send_sem=gsend.at[base + k - 1],
                    recv_sem=grecv.at[base + k - 1], device_id=target(k), device_id_type=MESH,
                )
            )
            copies[-1].start()
        for k in range(1, count):
            came_from = lax.rem(mine + count - k, count)
            pltpu.make_async_remote_copy(
                src_ref=seen.at[came_from], dst_ref=seen.at[came_from],
                send_sem=gsend.at[base + k - 1], recv_sem=grecv.at[base + k - 1],
                device_id=target(k), device_id_type=MESH,
            ).wait_recv()
        value = seen[0]
        for k in range(1, count):
            value = value + seen[k]
        gram_copies += copies
        base += count - 1
    gram_ref[...] = value

    @pl.loop(0, UNITS)
    def _(u):
        g, c = u // CHUNKS, lax.rem(u, CHUNKS)
        for level in range(3):
            for copy in y_copies(level, g, c) + x_copies(level, g, c):
                copy.wait_send()

    for level in range(3):
        for g in range(GROUPS):
            for up in (False, True):
                z_copy(level, g, up).wait_send()
    for copy in gram_copies:
        copy.wait_send()


def solve_kernel(filt, gram_ref, out_hbm, factor_ref, out, out_sem):
    def entry(i, j):
        at = NORB * (i % SUB) + j
        return jnp.broadcast_to(gram_ref[i // SUB : i // SUB + 1, at : at + 1], (SUB, LX))

    lower, inverse = {}, {}
    for j in range(NORB):
        column = {i: entry(i, j) for i in range(j, NORB)}
        for k in range(j):
            for i in range(j, NORB):
                column[i] = column[i] - lower[i, k] * lower[j, k]
        root = jnp.sqrt(column[j])
        scale = F32(1) / root
        lower[j, j] = root
        for i in range(j + 1, NORB):
            lower[i, j] = column[i] * scale
        for k in range(j):
            total = lower[j, k] * inverse[k, k]
            for m in range(k + 1, j):
                total = total + lower[j, m] * inverse[m, k]
            inverse[j, k] = -(total * scale)
        inverse[j, j] = scale

    row = lax.broadcasted_iota(jnp.int32, (SUB, LX), 0)
    lane = lax.broadcasted_iota(jnp.int32, (SUB, LX), 1)
    at_row = [row == i for i in range(SUB)]

    def gather(entries):
        halves = []
        for half in range(GROUPS):
            rows = jnp.zeros((SUB, LX), F32)
            for i in range(SUB):
                line = jnp.zeros((SUB, LX), F32)
                for j in range(NORB):
                    if (half * SUB + i, j) in entries:
                        line = jnp.where(lane == j, entries[half * SUB + i, j], line)
                rows = jnp.where(at_row[i], line, rows)
            halves.append(rows)
        return jnp.concatenate(halves, axis=0)

    high, low = split(gather(inverse)[:, :NORB])
    lhs = jnp.concatenate([high, high, low], axis=1)

    flat = out.reshape(NORB * ROWS, LX)

    def out_copy(c):
        part = pl.ds(c * SLABS * LY, SLABS * LY)
        return pltpu.make_async_copy(out.at[:, part], out_hbm.at[:, part], out_sem.at[c])

    for c in range(CHUNKS):
        @pl.loop(0, SLABS)
        def _(s, c=c):
            z = c * SLABS + s
            wide = jnp.concatenate(
                [
                    jnp.concatenate([filt[g, z, y] for g in range(GROUPS)], axis=0)
                    for y in range(LY)
                ],
                axis=1,
            )
            high, low = split(wide)
            solved = jnp.dot(
                lhs, jnp.concatenate([high, low, high], axis=0), preferred_element_type=F32
            )
            for y in range(LY):
                flat[pl.ds(z * LY + y, NORB, stride=ROWS), :] = solved[:, y * LX : (y + 1) * LX]

        out_copy(c).start()
    factor_ref[...] = gather({(j, i): value for (i, j), value in lower.items()})[:, :NORB]
    for c in range(CHUNKS):
        out_copy(c).wait()


def on_device(orbitals, potential):
    hbm = pl.BlockSpec(memory_space=pltpu.HBM)
    vmem = pl.BlockSpec(memory_space=pltpu.VMEM)
    dma = pltpu.SemaphoreType.DMA
    sizes = {axis: lax.axis_size(axis) for axis in AXES}
    partners = sizes["gx"] * sizes["gy"] + sizes["gz"] - 2
    filtered, gram = pl.pallas_call(
        filter_kernel,
        name="filter_and_gram",
        out_shape=[
            jax.ShapeDtypeStruct((GROUPS, LZ, LY, SUB, LX), F32),
            jax.ShapeDtypeStruct((2, LX), F32),
        ],
        in_specs=[hbm] * 3,
        out_specs=[vmem, vmem],
        scratch_shapes=[
            pltpu.VMEM((NORB, ROWS, LX), F32),
            pltpu.VMEM((3, GROUPS, LZ + 2 * HALO, LY + 2 * HALO, SUB, LX), F32),
            pltpu.VMEM((3, GROUPS, LZ, SUB, LX), F32),
            pltpu.VMEM((3, GROUPS, LZ, SUB, LX), F32),
            pltpu.VMEM((3, GROUPS, LZ, SUB, LX), F32),
            pltpu.VMEM((LZ, LY, LX), F32),
            pltpu.VMEM((2 * LX, 2 * LX), BF16),
            pltpu.VMEM((NORB, LX), F32),
            pltpu.VMEM((sizes["gx"] * sizes["gy"], 2, LX), F32),
            pltpu.VMEM((sizes["gz"], 2, LX), F32),
            dma((UNITS,)),
            dma((2,)),
            dma((3, UNITS, 2)),
            dma((3, UNITS, 2)),
            dma((3, UNITS, 2)),
            dma((3, UNITS, 2)),
            dma((3, GROUPS, 2)),
            dma((3, GROUPS, 2)),
            dma((partners,)),
            dma((partners,)),
        ],
        compiler_params=pltpu.CompilerParams(
            collective_id=0, has_side_effects=True, vmem_limit_bytes=40 * 2**20
        ),
        cost_estimate=pl.CostEstimate(
            flops=10**9, bytes_accessed=5 * 2**20, transcendentals=0
        ),
    )(*[
        pltpu.with_memory_space_constraint(value, pltpu.HBM)
        for value in (
            orbitals.reshape(NORB, ROWS, LX), potential, jnp.asarray(x_weights())
        )
    ])
    solved, factor = pl.pallas_call(
        solve_kernel,
        name="solve",
        out_shape=[
            jax.ShapeDtypeStruct((NORB, ROWS, LX), F32),
            jax.ShapeDtypeStruct((NORB, NORB), F32),
        ],
        in_specs=[vmem, vmem],
        out_specs=[hbm, vmem],
        scratch_shapes=[
            pltpu.VMEM((NORB, ROWS, LX), F32),
            dma((CHUNKS,)),
        ],
        compiler_params=pltpu.CompilerParams(vmem_limit_bytes=24 * 2**20),
        cost_estimate=pl.CostEstimate(
            flops=10**8, bytes_accessed=4 * 2**20, transcendentals=0
        ),
    )(filtered, gram)
    return solved.reshape(NORB, LZ, LY, LX), factor


def solution(mesh):
    in_specs = (P(None, "gz", "gy", "gx"), P("gz", "gy", "gx"))
    out_specs = (P(None, "gz", "gy", "gx"), P())
    return jax.shard_map(
        on_device, mesh=mesh, in_specs=in_specs, out_specs=out_specs, check_vma=False
    )
```

```python
import functools

import jax
import jax.numpy as jnp
import ml_dtypes
import numpy as np
from jax import lax
from jax.experimental import pallas as pl
from jax.experimental.pallas import tpu as pltpu
from jax.sharding import PartitionSpec as P

COEFFS = (-205.0 / 72.0, 8.0 / 5.0, -1.0 / 5.0, 8.0 / 315.0, -1.0 / 560.0)
SCALE = 2.0 * -2.0 / 20.0
TAPS = tuple(SCALE * c for c in COEFFS)

NORB, LZ, LY, LX = 16, 16, 16, 128
HALO = 4
SUB = 8
GROUPS = NORB // SUB
SLABS = 4
CHUNKS = LZ // SLABS
UNITS = GROUPS * CHUNKS
QUAD = 8 * HALO
UNROLL = 4
ROWS = LZ * LY
CELLS = 4194304
F32, BF16 = jnp.float32, jnp.bfloat16
MESH = pl.DeviceIdType.MESH
AXES = ("gx", "gy", "gz")


def x_weights():
    places = np.concatenate([np.arange(LX), np.arange(-HALO, 0), np.arange(LX, LX + HALO)])
    away = np.abs(places[:, None] - np.arange(LX)[None, :])
    full = np.zeros((LX + 2 * HALO, LX), np.float32)
    for k in range(1, HALO + 1):
        full[away == k] = np.float32(TAPS[k])
    high = full.astype(ml_dtypes.bfloat16)
    low = (full - high.astype(np.float32)).astype(ml_dtypes.bfloat16)
    halo = np.zeros((LX, LX), ml_dtypes.bfloat16)
    for start, part in ((0, high), (QUAD, high), (2 * QUAD, low)):
        halo[start : start + 2 * HALO] = part[LX:]
    return np.concatenate([high[:LX], halo, high[:LX], low[:LX]], axis=0)


def split(value):
    high = value.astype(BF16)
    return high, (value - high.astype(F32)).astype(BF16)


def filter_kernel(
    orb_hbm, pot_hbm, w_hbm, last, gram_ref,
    load, buf0, buf1, buf2, pack0, pack1, pack2, from_left, from_right, pv, w_ref, part, seen_xy, seen_z,
    load_sem, small_sem, ysend, yrecv, xsend, xrecv, zsend, zrecv, gsend, grecv,
):
    bufs, packs = (buf0, buf1, buf2), (pack0, pack1, pack2)
    sizes = {axis: lax.axis_size(axis) for axis in AXES}
    here = {axis: lax.axis_index(axis) for axis in AXES}

    def at(axis, step):
        return {axis: lax.rem(here[axis] + (step + sizes[axis]), sizes[axis])}

    def load_copy(g, c):
        part = (pl.ds(g * SUB, SUB), pl.ds(c * SLABS * LY, SLABS * LY))
        return pltpu.make_async_copy(
            orb_hbm.at[part], load.at[part], load_sem.at[g * CHUNKS + c]
        )

    small = [
        pltpu.make_async_copy(pot_hbm, pv, small_sem.at[0]),
        pltpu.make_async_copy(w_hbm, w_ref, small_sem.at[1]),
    ]
    for g in range(GROUPS):
        for c in range(CHUNKS):
            load_copy(g, c).start()
    for copy in small:
        copy.start()

    def in_plane(k):
        other = lax.rem(here["gx"] * sizes["gy"] + here["gy"] + k, sizes["gx"] * sizes["gy"])
        return {"gx": other // sizes["gy"], "gy": lax.rem(other, sizes["gy"])}

    def in_column(k):
        return at("gz", k)

    others = [in_plane(k) for k in range(1, sizes["gx"] * sizes["gy"])]
    others += [in_column(k) for k in range(1, sizes["gz"])]
    barrier = pltpu.get_barrier_semaphore()
    for device in others:
        pl.semaphore_signal(barrier, inc=1, device_id=device, device_id_type=MESH)

    def remote(src, dst, send_sem, recv_sem, axis, step):
        return pltpu.make_async_remote_copy(
            src_ref=src, dst_ref=dst, send_sem=send_sem, recv_sem=recv_sem,
            device_id=at(axis, step), device_id_type=MESH,
        )

    def y_copies(level, g, c):
        u, zs = g * CHUNKS + c, pl.ds(HALO + c * SLABS, SLABS)
        level_buf = bufs[level].at[g, zs]
        return [
            remote(
                level_buf.at[:, pl.ds(LY, HALO)], level_buf.at[:, pl.ds(0, HALO)],
                ysend.at[level, u, 0], yrecv.at[level, u, 0], "gy", 1,
            ),
            remote(
                level_buf.at[:, pl.ds(HALO, HALO)], level_buf.at[:, pl.ds(HALO + LY, HALO)],
                ysend.at[level, u, 1], yrecv.at[level, u, 1], "gy", -1,
            ),
        ]

    def x_copies(level, g, c):
        u, zs = g * CHUNKS + c, pl.ds(c * SLABS, SLABS)
        return [
            remote(
                packs[level].at[g, zs], from_left.at[level, g, zs],
                xsend.at[level, u, 0], xrecv.at[level, u, 0], "gx", 1,
            ),
            remote(
                packs[level].at[g, zs], from_right.at[level, g, zs],
                xsend.at[level, u, 1], xrecv.at[level, u, 1], "gx", -1,
            ),
        ]

    def z_copy(level, g, up):
        inner = pl.ds(HALO, LY)
        src, dst = (LZ, 0) if up else (HALO, HALO + LZ)
        i = 0 if up else 1
        return remote(
            bufs[level].at[g, pl.ds(src, HALO), inner],
            bufs[level].at[g, pl.ds(dst, HALO), inner],
            zsend.at[level, g, i], zrecv.at[level, g, i], "gz", 1 if up else -1,
        )

    def send(level, g, c):
        for copy in y_copies(level, g, c):
            copy.start()

        @pl.when(c == 0)
        def _():
            z_copy(level, g, False).start()

        @pl.when(c == CHUNKS - 1)
        def _():
            z_copy(level, g, True).start()

        for copy in x_copies(level, g, c):
            copy.start()

    lane = lax.broadcasted_iota(jnp.int32, (SUB, LX), 1)

    def pack_edges(values):
        packed = jnp.zeros((SUB, LX), F32)
        for y in range(LY):
            moved = pltpu.roll(values[y], 2 * HALO * y + HALO, 1)
            mine = (lane >= 2 * HALO * y) & (lane < 2 * HALO * (y + 1))
            packed = jnp.where(mine, moved, packed)
        return packed

    flat = load.reshape(NORB * ROWS, LX)

    def start_unit(g, c):
        load_copy(g, c).wait()

        @pl.loop(0, SLABS, unroll=UNROLL)
        def _(s):
            z = c * SLABS + s
            values = []
            for y in range(LY):
                v = flat[pl.ds(g * SUB * ROWS + z * LY + y, SUB, stride=ROWS), :]
                buf0[g, HALO + z, HALO + y] = v
                values.append(v)
            pack0[g, z] = pack_edges(values)

    start_unit(0, 0)
    pl.semaphore_wait(barrier, len(others))
    send(0, 0, 0)

    @pl.loop(1, UNITS)
    def _(u):
        g, c = u // CHUNKS, lax.rem(u, CHUNKS)
        start_unit(g, c)
        send(0, g, c)

    for copy in small:
        copy.wait()
    pv[...] = pv[...] * F32(0.1) + F32(3.0 * TAPS[0] - 2.3)

    def stencil(level, g, z):
        buf = bufs[level]
        edges = jnp.where(
            lax.rem(lane, 2 * HALO) < HALO, from_left[level, g, z], from_right[level, g, z]
        )
        edge_high = edges.astype(BF16).astype(F32)
        parts = (
            edge_high,
            pltpu.roll(edges - edge_high, QUAD, 1),
            pltpu.roll(edge_high, 2 * QUAD, 1),
        )
        halo = []
        for quad in range(LX // QUAD):
            own = parts[2]
            for i in (1, 0):
                own = jnp.where(lane // QUAD == (quad + i) % (LX // QUAD), parts[i], own)
            for y in range(QUAD // 8 * quad, QUAD // 8 * (quad + 1)):
                halo.append(pltpu.roll(own, (LX - 2 * HALO * y) % LX, 1))
        centre = [buf[g, HALO + z, HALO + y] for y in range(LY)]
        high, low = split(jnp.concatenate(centre, axis=0))
        rows = jnp.concatenate(
            [high, jnp.concatenate(halo, axis=0).astype(BF16), low, high], axis=1
        )
        along_x = jnp.dot(rows, w_ref[...], preferred_element_type=F32)
        out = []
        for y in range(LY):
            total = pv[z, pl.ds(y, 1), :] * centre[y] + along_x[y * SUB : (y + 1) * SUB]
            for k in range(1, HALO + 1):
                around = (
                    buf[g, HALO + z + k, HALO + y] + buf[g, HALO + z - k, HALO + y]
                ) + (buf[g, HALO + z, HALO + y + k] + buf[g, HALO + z, HALO + y - k])
                total = total + F32(TAPS[k]) * around
            out.append(total)
        return out

    def wait_halos(level, g, c):
        for copy in y_copies(level, g, c) + x_copies(level, g, c):
            copy.wait_recv()

        @pl.when(c == 0)
        def _():
            z_copy(level, g, True).wait_recv()

        @pl.when(c == CHUNKS - 1)
        def _():
            z_copy(level, g, False).wait_recv()

    for level in (1, 2):

        @pl.loop(0, UNITS)
        def _(u, level=level):
            g, c = u // CHUNKS, lax.rem(u, CHUNKS)
            wait_halos(level - 1, g, c)

            @pl.loop(0, SLABS, unroll=UNROLL)
            def _(s):
                z = c * SLABS + s
                new = stencil(level - 1, g, z)
                if level == 1:
                    new = [F32(0.5) * v for v in new]
                else:
                    new = [v - buf0[g, HALO + z, HALO + y] for y, v in enumerate(new)]
                for y in range(LY):
                    bufs[level][g, HALO + z, HALO + y] = new[y]
                packs[level][g, z] = pack_edges(new)

            send(level, g, c)

    part[...] = jnp.zeros_like(part)

    @pl.loop(0, UNITS)
    def _(u):
        g, c = u // CHUNKS, lax.rem(u, CHUNKS)
        wait_halos(2, g, c)

        @pl.loop(0, SLABS, unroll=UNROLL)
        def _(s):
            z = c * SLABS + s
            new = stencil(2, g, z)
            for y in range(LY):
                last[g, z, y] = new[y] - buf1[g, HALO + z, HALO + y]

        @pl.when(g == GROUPS - 1)
        def _():
            @pl.loop(0, SLABS, unroll=UNROLL)
            def _(s):
                z = c * SLABS + s
                wide = jnp.concatenate(
                    [
                        jnp.concatenate([last[k, z, y] for k in range(GROUPS)], axis=0)
                        for y in range(LY)
                    ],
                    axis=1,
                )
                high, low = split(wide)
                both = jnp.concatenate([high, low], axis=0)
                quad = lax.dot_general(
                    both, both, (((1,), (1,)), ((), ())), preferred_element_type=F32
                )
                four = quad[:NORB] + quad[NORB:]
                part[:, :NORB] += four[:, :NORB] + four[:, NORB:]

    def wait_sends():
        @pl.loop(0, UNITS)
        def _(u):
            g, c = u // CHUNKS, lax.rem(u, CHUNKS)
            for level in range(3):
                for copy in y_copies(level, g, c) + x_copies(level, g, c):
                    copy.wait_send()

        for level in range(3):
            for g in range(GROUPS):
                for up in (False, True):
                    z_copy(level, g, up).wait_send()

    moved = pltpu.roll(part[...] * F32(1.0 / CELLS), 0, 1, stride=NORB, stride_axis=0)
    value = jnp.sum(moved.reshape(2, SUB, LX), axis=1)
    plane = sizes["gx"] * sizes["gy"]
    stages = (
        (seen_xy, plane, here["gx"] * sizes["gy"] + here["gy"], in_plane),
        (seen_z, sizes["gz"], here["gz"], in_column),
    )
    for stage, (seen, count, mine, target) in enumerate(stages):
        seen[mine] = value
        for k in range(1, count):
            pltpu.make_async_remote_copy(
                src_ref=seen.at[mine], dst_ref=seen.at[mine], send_sem=gsend.at[stage],
                recv_sem=grecv.at[stage], device_id=target(k), device_id_type=MESH,
            ).start()
        if stage == 0:
            wait_sends()
        others = seen.at[pl.ds(0, count - 1)]
        pltpu.make_async_copy(others, others, grecv.at[stage]).wait()
        value = seen[0]
        for k in range(1, count):
            value = value + seen[k]
    gram_ref[...] = value
    for stage, (seen, count, _, _) in enumerate(stages):
        others = seen.at[pl.ds(0, count - 1)]
        pltpu.make_async_copy(others, others, gsend.at[stage]).wait()


def solve_kernel(filt, gram_ref, out_hbm, factor_ref, out, out_sem):
    def entry(i, j):
        at = NORB * (i % SUB) + j
        return jnp.broadcast_to(gram_ref[i // SUB : i // SUB + 1, at : at + 1], (SUB, LX))

    lower, inverse = {}, {}
    for j in range(NORB):
        column = {i: entry(i, j) for i in range(j, NORB)}
        for k in range(j):
            for i in range(j, NORB):
                column[i] = column[i] - lower[i, k] * lower[j, k]
        root = jnp.sqrt(column[j])
        scale = F32(1) / root
        lower[j, j] = root
        for i in range(j + 1, NORB):
            lower[i, j] = column[i] * scale
        for k in range(j):
            total = lower[j, k] * inverse[k, k]
            for m in range(k + 1, j):
                total = total + lower[j, m] * inverse[m, k]
            inverse[j, k] = -(total * scale)
        inverse[j, j] = scale

    row = lax.broadcasted_iota(jnp.int32, (SUB, LX), 0)
    lane = lax.broadcasted_iota(jnp.int32, (SUB, LX), 1)
    at_row = [row == i for i in range(SUB)]

    def gather(entries):
        halves = []
        for half in range(GROUPS):
            rows = jnp.zeros((SUB, LX), F32)
            for i in range(SUB):
                line = jnp.zeros((SUB, LX), F32)
                for j in range(NORB):
                    if (half * SUB + i, j) in entries:
                        line = jnp.where(lane == j, entries[half * SUB + i, j], line)
                rows = jnp.where(at_row[i], line, rows)
            halves.append(rows)
        return jnp.concatenate(halves, axis=0)

    high, low = split(gather(inverse)[:, :NORB])
    lhs = jnp.concatenate([high, high, low], axis=1)

    flat = out.reshape(NORB * ROWS, LX)

    def out_copy(c):
        part = pl.ds(c * SLABS * LY, SLABS * LY)
        return pltpu.make_async_copy(out.at[:, part], out_hbm.at[:, part], out_sem.at[c])

    for c in range(CHUNKS):
        @pl.loop(0, SLABS, unroll=UNROLL)
        def _(s, c=c):
            z = c * SLABS + s
            wide = jnp.concatenate(
                [
                    jnp.concatenate([filt[g, z, y] for g in range(GROUPS)], axis=0)
                    for y in range(LY)
                ],
                axis=1,
            )
            high, low = split(wide)
            solved = jnp.dot(
                lhs, jnp.concatenate([high, low, high], axis=0), preferred_element_type=F32
            )
            for y in range(LY):
                flat[pl.ds(z * LY + y, NORB, stride=ROWS), :] = solved[:, y * LX : (y + 1) * LX]

        out_copy(c).start()
    factor_ref[...] = gather({(j, i): value for (i, j), value in lower.items()})[:, :NORB]
    for c in range(CHUNKS):
        out_copy(c).wait()


def on_device(orbitals, potential):
    hbm = pl.BlockSpec(memory_space=pltpu.HBM)
    vmem = pl.BlockSpec(memory_space=pltpu.VMEM)
    dma = pltpu.SemaphoreType.DMA
    sizes = {axis: lax.axis_size(axis) for axis in AXES}
    filtered, gram = pl.pallas_call(
        filter_kernel,
        name="filter_and_gram",
        out_shape=[
            jax.ShapeDtypeStruct((GROUPS, LZ, LY, SUB, LX), F32),
            jax.ShapeDtypeStruct((2, LX), F32),
        ],
        in_specs=[hbm] * 3,
        out_specs=[vmem, vmem],
        scratch_shapes=[
            pltpu.VMEM((NORB, ROWS, LX), F32),
            *[pltpu.VMEM((GROUPS, LZ + 2 * HALO, LY + 2 * HALO, SUB, LX), F32)] * 3,
            *[pltpu.VMEM((GROUPS, LZ, SUB, LX), F32)] * 3,
            *[pltpu.VMEM((3, GROUPS, LZ, SUB, LX), F32)] * 2,
            pltpu.VMEM((LZ, LY, LX), F32),
            pltpu.VMEM((4 * LX, LX), BF16),
            pltpu.VMEM((NORB, LX), F32),
            pltpu.VMEM((sizes["gx"] * sizes["gy"], 2, LX), F32),
            pltpu.VMEM((sizes["gz"], 2, LX), F32),
            dma((UNITS,)),
            dma((2,)),
            dma((3, UNITS, 2)),
            dma((3, UNITS, 2)),
            dma((3, UNITS, 2)),
            dma((3, UNITS, 2)),
            dma((3, GROUPS, 2)),
            dma((3, GROUPS, 2)),
            dma((2,)),
            dma((2,)),
        ],
        compiler_params=pltpu.CompilerParams(
            collective_id=0, has_side_effects=True, vmem_limit_bytes=40 * 2**20
        ),
        cost_estimate=pl.CostEstimate(
            flops=10**9, bytes_accessed=5 * 2**20, transcendentals=0
        ),
    )(*[
        pltpu.with_memory_space_constraint(value, pltpu.HBM)
        for value in (
            orbitals.reshape(NORB, ROWS, LX), potential, jnp.asarray(x_weights())
        )
    ])
    solved, factor = pl.pallas_call(
        solve_kernel,
        name="solve",
        out_shape=[
            jax.ShapeDtypeStruct((NORB, ROWS, LX), F32),
            jax.ShapeDtypeStruct((NORB, NORB), F32),
        ],
        in_specs=[vmem, vmem],
        out_specs=[hbm, vmem],
        scratch_shapes=[
            pltpu.VMEM((NORB, ROWS, LX), F32),
            dma((CHUNKS,)),
        ],
        compiler_params=pltpu.CompilerParams(vmem_limit_bytes=24 * 2**20),
        cost_estimate=pl.CostEstimate(
            flops=10**8, bytes_accessed=4 * 2**20, transcendentals=0
        ),
    )(filtered, gram)
    return solved.reshape(NORB, LZ, LY, LX), factor


def solution(mesh):
    in_specs = (P(None, "gz", "gy", "gx"), P("gz", "gy", "gx"))
    out_specs = (P(None, "gz", "gy", "gx"), P())
    return jax.shard_map(
        on_device, mesh=mesh, in_specs=in_specs, out_specs=out_specs, check_vma=False
    )
```

```python
import functools

import jax
import jax.numpy as jnp
import ml_dtypes
import numpy as np
from jax import lax
from jax.experimental import pallas as pl
from jax.experimental.pallas import tpu as pltpu
from jax.sharding import PartitionSpec as P

COEFFS = (-205.0 / 72.0, 8.0 / 5.0, -1.0 / 5.0, 8.0 / 315.0, -1.0 / 560.0)
SCALE = 2.0 * -2.0 / 20.0
TAPS = tuple(SCALE * c for c in COEFFS)

NORB, LZ, LY, LX = 16, 16, 16, 128
HALO = 4
SUB = 8
GROUPS = NORB // SUB
SLABS = 4
CHUNKS = LZ // SLABS
UNITS = GROUPS * CHUNKS
QUAD = 8 * HALO
UNROLL = 4
STEP = 2
ROWS = LZ * LY
CELLS = 4194304
F32, BF16 = jnp.float32, jnp.bfloat16
MESH = pl.DeviceIdType.MESH
AXES = ("gx", "gy", "gz")


def x_weights():
    places = np.concatenate([np.arange(LX), np.arange(-HALO, 0), np.arange(LX, LX + HALO)])
    away = np.abs(places[:, None] - np.arange(LX)[None, :])
    full = np.zeros((LX + 2 * HALO, LX), np.float32)
    for k in range(1, HALO + 1):
        full[away == k] = np.float32(TAPS[k])
    high = full.astype(ml_dtypes.bfloat16)
    low = (full - high.astype(np.float32)).astype(ml_dtypes.bfloat16)
    halo = np.zeros((LX, LX), ml_dtypes.bfloat16)
    for start, part in ((0, high), (QUAD, high), (2 * QUAD, low)):
        halo[start : start + 2 * HALO] = part[LX:]
    return np.concatenate([high[:LX], halo, high[:LX], low[:LX]], axis=0)


def split(value):
    high = value.astype(BF16)
    return high, (value - high.astype(F32)).astype(BF16)


def filter_kernel(
    orb_hbm, pot_hbm, w_hbm, last, gram_ref,
    load, buf0, buf1, buf2, pack0, pack1, pack2, from_left, from_right, pv, w_ref, part, seen_xy, seen_z,
    load_sem, small_sem, ysend, yrecv, xsend, xrecv, zsend, zrecv, gsend, grecv,
):
    bufs, packs = (buf0, buf1, buf2), (pack0, pack1, pack2)
    sizes = {axis: lax.axis_size(axis) for axis in AXES}
    here = {axis: lax.axis_index(axis) for axis in AXES}

    def at(axis, step):
        return {axis: lax.rem(here[axis] + (step + sizes[axis]), sizes[axis])}

    neighbours = [(axis, step) for axis in ("gy", "gz", "gx") for step in (1, -1)]
    barrier = pltpu.get_barrier_semaphore()
    for axis, step in neighbours:
        pl.semaphore_signal(barrier, inc=1, device_id=at(axis, step), device_id_type=MESH)

    def in_plane(k):
        other = lax.rem(here["gx"] * sizes["gy"] + here["gy"] + k, sizes["gx"] * sizes["gy"])
        return {"gx": other // sizes["gy"], "gy": lax.rem(other, sizes["gy"])}

    def in_column(k):
        return at("gz", k)

    def load_copy(g, c):
        part = (pl.ds(g * SUB, SUB), pl.ds(c * SLABS * LY, SLABS * LY))
        return pltpu.make_async_copy(
            orb_hbm.at[part], load.at[part], load_sem.at[g * CHUNKS + c]
        )

    small = [
        pltpu.make_async_copy(pot_hbm, pv, small_sem.at[0]),
        pltpu.make_async_copy(w_hbm, w_ref, small_sem.at[1]),
    ]
    for g in range(GROUPS):
        for c in range(CHUNKS):
            load_copy(g, c).start()
    for copy in small:
        copy.start()

    def remote(src, dst, send_sem, recv_sem, axis, step):
        return pltpu.make_async_remote_copy(
            src_ref=src, dst_ref=dst, send_sem=send_sem, recv_sem=recv_sem,
            device_id=at(axis, step), device_id_type=MESH,
        )

    def y_copies(level, g, c):
        u, zs = g * CHUNKS + c, pl.ds(HALO + c * SLABS, SLABS)
        level_buf = bufs[level].at[g, zs]
        return [
            remote(
                level_buf.at[:, pl.ds(LY, HALO)], level_buf.at[:, pl.ds(0, HALO)],
                ysend.at[level, u, 0], yrecv.at[level, u, 0], "gy", 1,
            ),
            remote(
                level_buf.at[:, pl.ds(HALO, HALO)], level_buf.at[:, pl.ds(HALO + LY, HALO)],
                ysend.at[level, u, 1], yrecv.at[level, u, 1], "gy", -1,
            ),
        ]

    def x_copies(level, g, c):
        u, zs = g * CHUNKS + c, pl.ds(c * SLABS, SLABS)
        return [
            remote(
                packs[level].at[g, zs], from_left.at[level, g, zs],
                xsend.at[level, u, 0], xrecv.at[level, u, 0], "gx", 1,
            ),
            remote(
                packs[level].at[g, zs], from_right.at[level, g, zs],
                xsend.at[level, u, 1], xrecv.at[level, u, 1], "gx", -1,
            ),
        ]

    def z_copy(level, g, up):
        inner = pl.ds(HALO, LY)
        src, dst = (LZ, 0) if up else (HALO, HALO + LZ)
        i = 0 if up else 1
        return remote(
            bufs[level].at[g, pl.ds(src, HALO), inner],
            bufs[level].at[g, pl.ds(dst, HALO), inner],
            zsend.at[level, g, i], zrecv.at[level, g, i], "gz", 1 if up else -1,
        )

    def send(level, g, c):
        for copy in y_copies(level, g, c):
            copy.start()

        @pl.when(c == 0)
        def _():
            z_copy(level, g, False).start()

        @pl.when(c == CHUNKS - 1)
        def _():
            z_copy(level, g, True).start()

        for copy in x_copies(level, g, c):
            copy.start()

    lane = lax.broadcasted_iota(jnp.int32, (SUB, LX), 1)

    def pack_edges(values):
        packed = jnp.zeros((SUB, LX), F32)
        for y in range(LY):
            moved = pltpu.roll(values[y], 2 * HALO * y + HALO, 1)
            mine = (lane >= 2 * HALO * y) & (lane < 2 * HALO * (y + 1))
            packed = jnp.where(mine, moved, packed)
        return packed

    flat = load.reshape(NORB * ROWS, LX)

    def start_unit(g, c):
        load_copy(g, c).wait()

        @pl.loop(0, SLABS, unroll=UNROLL)
        def _(s):
            z = c * SLABS + s
            values = []
            for y in range(LY):
                v = flat[pl.ds(g * SUB * ROWS + z * LY + y, SUB, stride=ROWS), :]
                buf0[g, HALO + z, HALO + y] = v
                values.append(v)
            pack0[g, z] = pack_edges(values)

    start_unit(0, 0)
    pl.semaphore_wait(barrier, len(neighbours))
    send(0, 0, 0)

    @pl.loop(1, UNITS)
    def _(u):
        g, c = u // CHUNKS, lax.rem(u, CHUNKS)
        start_unit(g, c)
        send(0, g, c)

    for copy in small:
        copy.wait()
    pv[...] = pv[...] * F32(0.1) + F32(3.0 * TAPS[0] - 2.3)

    def stencil(level, g, z):
        buf = bufs[level]
        edges = jnp.where(
            lax.rem(lane, 2 * HALO) < HALO, from_left[level, g, z], from_right[level, g, z]
        )
        edge_high = edges.astype(BF16).astype(F32)
        parts = (
            edge_high,
            pltpu.roll(edges - edge_high, QUAD, 1),
            pltpu.roll(edge_high, 2 * QUAD, 1),
        )
        halo = []
        for quad in range(LX // QUAD):
            own = parts[2]
            for i in (1, 0):
                own = jnp.where(lane // QUAD == (quad + i) % (LX // QUAD), parts[i], own)
            for y in range(QUAD // 8 * quad, QUAD // 8 * (quad + 1)):
                halo.append(pltpu.roll(own, (LX - 2 * HALO * y) % LX, 1))
        centre = [buf[g, HALO + z, HALO + y] for y in range(LY)]
        high, low = split(jnp.concatenate(centre, axis=0))
        rows = jnp.concatenate(
            [high, jnp.concatenate(halo, axis=0).astype(BF16), low, high], axis=1
        )
        along_x = jnp.dot(rows, w_ref[...], preferred_element_type=F32)
        out = []
        for y in range(LY):
            total = pv[z, pl.ds(y, 1), :] * centre[y] + along_x[y * SUB : (y + 1) * SUB]
            for k in range(1, HALO + 1):
                around = (
                    buf[g, HALO + z + k, HALO + y] + buf[g, HALO + z - k, HALO + y]
                ) + (buf[g, HALO + z, HALO + y + k] + buf[g, HALO + z, HALO + y - k])
                total = total + F32(TAPS[k]) * around
            out.append(total)
        return out

    def wait_halos(level, g, c):
        for copy in y_copies(level, g, c) + x_copies(level, g, c):
            copy.wait_recv()

        @pl.when(c == 0)
        def _():
            z_copy(level, g, True).wait_recv()

        @pl.when(c == CHUNKS - 1)
        def _():
            z_copy(level, g, False).wait_recv()

    for level in (1, 2):

        @pl.loop(0, UNITS)
        def _(u, level=level):
            g, c = u // CHUNKS, lax.rem(u, CHUNKS)
            wait_halos(level - 1, g, c)

            @pl.loop(0, SLABS, unroll=UNROLL)
            def _(s):
                z = c * SLABS + s
                new = stencil(level - 1, g, z)
                if level == 1:
                    new = [F32(0.5) * v for v in new]
                else:
                    new = [v - buf0[g, HALO + z, HALO + y] for y, v in enumerate(new)]
                for y in range(LY):
                    bufs[level][g, HALO + z, HALO + y] = new[y]
                packs[level][g, z] = pack_edges(new)

            send(level, g, c)

    part[...] = jnp.zeros_like(part)

    @pl.loop(0, UNITS)
    def _(u):
        g, c = u // CHUNKS, lax.rem(u, CHUNKS)
        wait_halos(2, g, c)

        @pl.loop(0, SLABS, unroll=UNROLL)
        def _(s):
            z = c * SLABS + s
            new = stencil(2, g, z)
            for y in range(LY):
                last[g, z, y] = new[y] - buf1[g, HALO + z, HALO + y]

        @pl.when(g == GROUPS - 1)
        def _():
            @pl.loop(0, SLABS, unroll=UNROLL)
            def _(s):
                z = c * SLABS + s
                wide = jnp.concatenate(
                    [
                        jnp.concatenate([last[k, z, y] for k in range(GROUPS)], axis=0)
                        for y in range(LY)
                    ],
                    axis=1,
                )
                high, low = split(wide)
                both = jnp.concatenate([high, low], axis=0)
                quad = lax.dot_general(
                    both, both, (((1,), (1,)), ((), ())), preferred_element_type=F32
                )
                four = quad[:NORB] + quad[NORB:]
                part[:, :NORB] += four[:, :NORB] + four[:, NORB:]

    def wait_sends():
        @pl.loop(0, UNITS)
        def _(u):
            g, c = u // CHUNKS, lax.rem(u, CHUNKS)
            for level in range(3):
                for copy in y_copies(level, g, c) + x_copies(level, g, c):
                    copy.wait_send()

        for level in range(3):
            for g in range(GROUPS):
                for up in (False, True):
                    z_copy(level, g, up).wait_send()

    moved = pltpu.roll(part[...] * F32(1.0 / CELLS), 0, 1, stride=NORB, stride_axis=0)
    value = jnp.sum(moved.reshape(2, SUB, LX), axis=1)
    plane = sizes["gx"] * sizes["gy"]
    stages = (
        (seen_xy, plane, here["gx"] * sizes["gy"] + here["gy"], in_plane),
        (seen_z, sizes["gz"], here["gz"], in_column),
    )
    for stage, (seen, count, mine, target) in enumerate(stages):
        seen[mine] = value
        for k in range(1, count):
            pltpu.make_async_remote_copy(
                src_ref=seen.at[mine], dst_ref=seen.at[mine], send_sem=gsend.at[stage],
                recv_sem=grecv.at[stage], device_id=target(k), device_id_type=MESH,
            ).start()
        if stage == 0:
            wait_sends()
        others = seen.at[pl.ds(0, count - 1)]
        pltpu.make_async_copy(others, others, grecv.at[stage]).wait()
        value = seen[0]
        for k in range(1, count):
            value = value + seen[k]
    gram_ref[...] = value
    for stage, (seen, count, _, _) in enumerate(stages):
        others = seen.at[pl.ds(0, count - 1)]
        pltpu.make_async_copy(others, others, gsend.at[stage]).wait()


def solve_kernel(filt, gram_ref, out_hbm, factor_ref, out, out_sem):
    def entry(i, j):
        at = NORB * (i % SUB) + j
        return jnp.broadcast_to(gram_ref[i // SUB : i // SUB + 1, at : at + 1], (SUB, LX))

    row = lax.broadcasted_iota(jnp.int32, (SUB, LX), 0)
    lane = lax.broadcasted_iota(jnp.int32, (SUB, LX), 1)
    lower, inverse = {}, []
    for j in range(NORB):
        column = {i: entry(i, j) for i in range(j, NORB)}
        for k in range(j):
            for i in range(j, NORB):
                column[i] = column[i] - lower[i, k] * lower[j, k]
        root = jnp.sqrt(column[j])
        scale = F32(1) / root
        lower[j, j] = root
        for i in range(j + 1, NORB):
            lower[i, j] = column[i] * scale
        line = jnp.where(lane == j, F32(1), F32(0))
        for m in range(j):
            line = line - lower[j, m] * inverse[m]
        inverse.append(line * scale)

    def stack(lines):
        halves = []
        for half in range(GROUPS):
            rows = lines[half * SUB]
            for i in range(1, SUB):
                rows = jnp.where(row == i, lines[half * SUB + i], rows)
            halves.append(rows)
        return jnp.concatenate(halves, axis=0)

    def gather(entries):
        lines = []
        for i in range(NORB):
            line = jnp.zeros((SUB, LX), F32)
            for j in range(NORB):
                if (i, j) in entries:
                    line = jnp.where(lane == j, entries[i, j], line)
            lines.append(line)
        return stack(lines)

    high, low = split(stack(inverse)[:, :NORB])
    lhs = jnp.concatenate([high, high, low], axis=1)

    def out_copy(c):
        part = pl.ds(c * STEP * LY, STEP * LY)
        return pltpu.make_async_copy(out.at[:, part], out_hbm.at[:, part], out_sem.at[c])

    for c in range(LZ // STEP):
        for z in range(c * STEP, (c + 1) * STEP):
            wide = jnp.concatenate(
                [
                    jnp.concatenate([filt[g, z, y] for g in range(GROUPS)], axis=0)
                    for y in range(LY)
                ],
                axis=1,
            )
            high, low = split(wide)
            solved = jnp.dot(
                lhs, jnp.concatenate([high, low, high], axis=0), preferred_element_type=F32
            )
            for g in range(GROUPS):
                for start in range(0, LY, SUB):
                    block = jnp.stack(
                        [
                            solved[g * SUB : (g + 1) * SUB, y * LX : (y + 1) * LX]
                            for y in range(start, start + SUB)
                        ]
                    )
                    out[pl.ds(g * SUB, SUB), pl.ds(z * LY + start, SUB), :] = jnp.swapaxes(
                        block, 0, 1
                    )
        out_copy(c).start()
    factor_ref[...] = gather({(j, i): value for (i, j), value in lower.items()})[:, :NORB]
    for c in range(LZ // STEP):
        out_copy(c).wait()


def on_device(orbitals, potential):
    hbm = pl.BlockSpec(memory_space=pltpu.HBM)
    vmem = pl.BlockSpec(memory_space=pltpu.VMEM)
    dma = pltpu.SemaphoreType.DMA
    sizes = {axis: lax.axis_size(axis) for axis in AXES}
    filtered, gram = pl.pallas_call(
        filter_kernel,
        name="filter_and_gram",
        out_shape=[
            jax.ShapeDtypeStruct((GROUPS, LZ, LY, SUB, LX), F32),
            jax.ShapeDtypeStruct((2, LX), F32),
        ],
        in_specs=[hbm] * 3,
        out_specs=[vmem, vmem],
        scratch_shapes=[
            pltpu.VMEM((NORB, ROWS, LX), F32),
            *[pltpu.VMEM((GROUPS, LZ + 2 * HALO, LY + 2 * HALO, SUB, LX), F32)] * 3,
            *[pltpu.VMEM((GROUPS, LZ, SUB, LX), F32)] * 3,
            *[pltpu.VMEM((3, GROUPS, LZ, SUB, LX), F32)] * 2,
            pltpu.VMEM((LZ, LY, LX), F32),
            pltpu.VMEM((4 * LX, LX), BF16),
            pltpu.VMEM((NORB, LX), F32),
            pltpu.VMEM((sizes["gx"] * sizes["gy"], 2, LX), F32),
            pltpu.VMEM((sizes["gz"], 2, LX), F32),
            dma((UNITS,)),
            dma((2,)),
            dma((3, UNITS, 2)),
            dma((3, UNITS, 2)),
            dma((3, UNITS, 2)),
            dma((3, UNITS, 2)),
            dma((3, GROUPS, 2)),
            dma((3, GROUPS, 2)),
            dma((2,)),
            dma((2,)),
        ],
        compiler_params=pltpu.CompilerParams(
            collective_id=0, has_side_effects=True, vmem_limit_bytes=40 * 2**20
        ),
        cost_estimate=pl.CostEstimate(
            flops=10**9, bytes_accessed=5 * 2**20, transcendentals=0
        ),
    )(*[
        pltpu.with_memory_space_constraint(value, pltpu.HBM)
        for value in (
            orbitals.reshape(NORB, ROWS, LX), potential, jnp.asarray(x_weights())
        )
    ])
    solved, factor = pl.pallas_call(
        solve_kernel,
        name="solve",
        out_shape=[
            jax.ShapeDtypeStruct((NORB, ROWS, LX), F32),
            jax.ShapeDtypeStruct((NORB, NORB), F32),
        ],
        in_specs=[vmem, vmem],
        out_specs=[hbm, vmem],
        scratch_shapes=[
            pltpu.VMEM((NORB, ROWS, LX), F32),
            dma((LZ // STEP,)),
        ],
        compiler_params=pltpu.CompilerParams(vmem_limit_bytes=24 * 2**20),
        cost_estimate=pl.CostEstimate(
            flops=10**8, bytes_accessed=4 * 2**20, transcendentals=0
        ),
    )(filtered, gram)
    return solved.reshape(NORB, LZ, LY, LX), factor


def solution(mesh):
    in_specs = (P(None, "gz", "gy", "gx"), P("gz", "gy", "gx"))
    out_specs = (P(None, "gz", "gy", "gx"), P())
    return jax.shard_map(
        on_device, mesh=mesh, in_specs=in_specs, out_specs=out_specs, check_vma=False
    )
```

```python
import functools

import jax
import jax.numpy as jnp
import ml_dtypes
import numpy as np
from jax import lax
from jax.experimental import pallas as pl
from jax.experimental.pallas import tpu as pltpu
from jax.sharding import PartitionSpec as P

COEFFS = (-205.0 / 72.0, 8.0 / 5.0, -1.0 / 5.0, 8.0 / 315.0, -1.0 / 560.0)
SCALE = 2.0 * -2.0 / 20.0
TAPS = tuple(SCALE * c for c in COEFFS)

NORB, LZ, LY, LX = 16, 16, 16, 128
HALO = 4
SUB = 8
GROUPS = NORB // SUB
SLABS = 4
CHUNKS = LZ // SLABS
UNITS = GROUPS * CHUNKS
QUAD = 8 * HALO
UNROLL = 4
STEP = 2
ROWS = LZ * LY
CELLS = 4194304
F32, BF16 = jnp.float32, jnp.bfloat16
MESH = pl.DeviceIdType.MESH
AXES = ("gx", "gy", "gz")


def x_weights():
    places = np.concatenate([np.arange(LX), np.arange(-HALO, 0), np.arange(LX, LX + HALO)])
    away = np.abs(places[:, None] - np.arange(LX)[None, :])
    full = np.zeros((LX + 2 * HALO, LX), np.float32)
    for k in range(1, HALO + 1):
        full[away == k] = np.float32(TAPS[k])
    high = full.astype(ml_dtypes.bfloat16)
    low = (full - high.astype(np.float32)).astype(ml_dtypes.bfloat16)
    halo = np.zeros((LX, LX), ml_dtypes.bfloat16)
    for start, part in ((0, high), (QUAD, high), (2 * QUAD, low)):
        halo[start : start + 2 * HALO] = part[LX:]
    return np.concatenate([high[:LX], halo, high[:LX], low[:LX]], axis=0)


def split(value):
    high = value.astype(BF16)
    return high, (value - high.astype(F32)).astype(BF16)


def filter_kernel(
    orb_hbm, pot_hbm, w_hbm, last, gram_ref,
    load, buf0, buf1, buf2, pack0, pack1, pack2, from_left, from_right, pv, w_ref, part, pair, seen, word,
    load_sem, small_sem, ysend, yrecv, xsend, xrecv, zsend, zrecv, gsend, grecv,
):
    bufs, packs = (buf0, buf1, buf2), (pack0, pack1, pack2)
    sizes = {axis: lax.axis_size(axis) for axis in AXES}
    here = {axis: lax.axis_index(axis) for axis in AXES}

    def at(axis, step):
        return {axis: lax.rem(here[axis] + (step + sizes[axis]), sizes[axis])}

    neighbours = [(axis, step) for axis in ("gy", "gz", "gx") for step in (1, -1)]
    barrier = pltpu.get_barrier_semaphore()
    for axis, step in neighbours:
        pl.semaphore_signal(barrier, inc=1, device_id=at(axis, step), device_id_type=MESH)

    def load_copy(g, c):
        part = (pl.ds(g * SUB, SUB), pl.ds(c * SLABS * LY, SLABS * LY))
        return pltpu.make_async_copy(
            orb_hbm.at[part], load.at[part], load_sem.at[g * CHUNKS + c]
        )

    small = [
        pltpu.make_async_copy(pot_hbm, pv, small_sem.at[0]),
        pltpu.make_async_copy(w_hbm, w_ref, small_sem.at[1]),
    ]
    for g in range(GROUPS):
        for c in range(CHUNKS):
            load_copy(g, c).start()
    for copy in small:
        copy.start()

    def remote(src, dst, send_sem, recv_sem, axis, step):
        return pltpu.make_async_remote_copy(
            src_ref=src, dst_ref=dst, send_sem=send_sem, recv_sem=recv_sem,
            device_id=at(axis, step), device_id_type=MESH,
        )

    def y_copies(level, g, c):
        u, zs = g * CHUNKS + c, pl.ds(HALO + c * SLABS, SLABS)
        level_buf = bufs[level].at[g, zs]
        return [
            remote(
                level_buf.at[:, pl.ds(LY, HALO)], level_buf.at[:, pl.ds(0, HALO)],
                ysend.at[level, u, 0], yrecv.at[level, u, 0], "gy", 1,
            ),
            remote(
                level_buf.at[:, pl.ds(HALO, HALO)], level_buf.at[:, pl.ds(HALO + LY, HALO)],
                ysend.at[level, u, 1], yrecv.at[level, u, 1], "gy", -1,
            ),
        ]

    def x_copies(level, g, c):
        u, zs = g * CHUNKS + c, pl.ds(c * SLABS, SLABS)
        return [
            remote(
                packs[level].at[g, zs], from_left.at[level, g, zs],
                xsend.at[level, u, 0], xrecv.at[level, u, 0], "gx", 1,
            ),
            remote(
                packs[level].at[g, zs], from_right.at[level, g, zs],
                xsend.at[level, u, 1], xrecv.at[level, u, 1], "gx", -1,
            ),
        ]

    def z_copy(level, g, up):
        inner = pl.ds(HALO, LY)
        src, dst = (LZ, 0) if up else (HALO, HALO + LZ)
        i = 0 if up else 1
        return remote(
            bufs[level].at[g, pl.ds(src, HALO), inner],
            bufs[level].at[g, pl.ds(dst, HALO), inner],
            zsend.at[level, g, i], zrecv.at[level, g, i], "gz", 1 if up else -1,
        )

    def send(level, g, c):
        for copy in y_copies(level, g, c):
            copy.start()

        @pl.when(c == 0)
        def _():
            z_copy(level, g, False).start()

        @pl.when(c == CHUNKS - 1)
        def _():
            z_copy(level, g, True).start()

        for copy in x_copies(level, g, c):
            copy.start()

    lane = lax.broadcasted_iota(jnp.int32, (SUB, LX), 1)

    def pack_edges(values):
        packed = jnp.zeros((SUB, LX), F32)
        for y in range(LY):
            moved = pltpu.roll(values[y], 2 * HALO * y + HALO, 1)
            mine = (lane >= 2 * HALO * y) & (lane < 2 * HALO * (y + 1))
            packed = jnp.where(mine, moved, packed)
        return packed

    flat = load.reshape(NORB * ROWS, LX)

    def start_unit(g, c):
        load_copy(g, c).wait()

        @pl.loop(0, SLABS, unroll=UNROLL)
        def _(s):
            z = c * SLABS + s
            values = []
            for y in range(LY):
                v = flat[pl.ds(g * SUB * ROWS + z * LY + y, SUB, stride=ROWS), :]
                buf0[g, HALO + z, HALO + y] = v
                values.append(v)
            pack0[g, z] = pack_edges(values)

    start_unit(0, 0)
    pl.semaphore_wait(barrier, len(neighbours))
    send(0, 0, 0)

    @pl.loop(1, UNITS)
    def _(u):
        g, c = u // CHUNKS, lax.rem(u, CHUNKS)
        start_unit(g, c)
        send(0, g, c)

    for copy in small:
        copy.wait()
    pv[...] = pv[...] * F32(0.1) + F32(3.0 * TAPS[0] - 2.3)

    def stencil(level, g, z):
        buf = bufs[level]
        edges = jnp.where(
            lax.rem(lane, 2 * HALO) < HALO, from_left[level, g, z], from_right[level, g, z]
        )
        edge_high = edges.astype(BF16).astype(F32)
        parts = (
            edge_high,
            pltpu.roll(edges - edge_high, QUAD, 1),
            pltpu.roll(edge_high, 2 * QUAD, 1),
        )
        halo = []
        for quad in range(LX // QUAD):
            own = parts[2]
            for i in (1, 0):
                own = jnp.where(lane // QUAD == (quad + i) % (LX // QUAD), parts[i], own)
            for y in range(QUAD // 8 * quad, QUAD // 8 * (quad + 1)):
                halo.append(pltpu.roll(own, (LX - 2 * HALO * y) % LX, 1))
        centre = [buf[g, HALO + z, HALO + y] for y in range(LY)]
        high, low = split(jnp.concatenate(centre, axis=0))
        rows = jnp.concatenate(
            [high, jnp.concatenate(halo, axis=0).astype(BF16), low, high], axis=1
        )
        along_x = jnp.dot(rows, w_ref[...], preferred_element_type=F32)
        out = []
        for y in range(LY):
            total = pv[z, pl.ds(y, 1), :] * centre[y] + along_x[y * SUB : (y + 1) * SUB]
            for k in range(1, HALO + 1):
                around = (
                    buf[g, HALO + z + k, HALO + y] + buf[g, HALO + z - k, HALO + y]
                ) + (buf[g, HALO + z, HALO + y + k] + buf[g, HALO + z, HALO + y - k])
                total = total + F32(TAPS[k]) * around
            out.append(total)
        return out

    def wait_halos(level, g, c):
        for copy in y_copies(level, g, c) + x_copies(level, g, c):
            copy.wait_recv()

        @pl.when(c == 0)
        def _():
            z_copy(level, g, True).wait_recv()

        @pl.when(c == CHUNKS - 1)
        def _():
            z_copy(level, g, False).wait_recv()

    core = lax.rem(here["gz"], 2)
    layers = sizes["gz"] // 2
    rounds = (
        [("gx", d) for d in range(1, sizes["gx"])],
        [("gy", d) for d in range(1, sizes["gy"])],
        [("gz", 2), ("gz", -2)],
        [("gz", d) for d in range(4, sizes["gz"] - 3, 2)],
    )

    def tell(i):
        for axis, step in rounds[i]:
            pl.semaphore_signal(
                word.at[i], inc=1, device_id=at(axis, step), device_id_type=MESH
            )

    def hear(i):
        pl.semaphore_wait(word.at[i], len(rounds[i]))

    for level in (1, 2):
        if level == 2:
            tell(0)

        @pl.loop(0, UNITS)
        def _(u, level=level):
            g, c = u // CHUNKS, lax.rem(u, CHUNKS)
            wait_halos(level - 1, g, c)

            if level == 2:

                @pl.when(u == CHUNKS)
                def _():
                    hear(0)
                    tell(1)

            @pl.loop(0, SLABS, unroll=UNROLL)
            def _(s):
                z = c * SLABS + s
                new = stencil(level - 1, g, z)
                if level == 1:
                    new = [F32(0.5) * v for v in new]
                else:
                    new = [v - buf0[g, HALO + z, HALO + y] for y, v in enumerate(new)]
                for y in range(LY):
                    bufs[level][g, HALO + z, HALO + y] = new[y]
                packs[level][g, z] = pack_edges(new)

            send(level, g, c)

    hear(1)
    tell(2)
    part[...] = jnp.zeros_like(part)

    @pl.loop(0, UNITS)
    def _(u):
        g, c = u // CHUNKS, lax.rem(u, CHUNKS)
        wait_halos(2, g, c)

        @pl.when(u == CHUNKS)
        def _():
            hear(2)
            tell(3)

        @pl.loop(0, SLABS, unroll=UNROLL)
        def _(s):
            z = c * SLABS + s
            new = stencil(2, g, z)
            for y in range(LY):
                last[g, z, y] = new[y] - buf1[g, HALO + z, HALO + y]

        @pl.when(g == GROUPS - 1)
        def _():
            @pl.loop(0, SLABS, unroll=UNROLL)
            def _(s):
                z = c * SLABS + s
                wide = jnp.concatenate(
                    [
                        jnp.concatenate([last[k, z, y] for k in range(GROUPS)], axis=0)
                        for y in range(LY)
                    ],
                    axis=1,
                )
                high, low = split(wide)
                both = jnp.concatenate([high, low], axis=0)
                quad = lax.dot_general(
                    both, both, (((1,), (1,)), ((), ())), preferred_element_type=F32
                )
                four = quad[:NORB] + quad[NORB:]
                part[:, :NORB] += four[:, :NORB] + four[:, NORB:]

    def wait_sends():
        @pl.loop(0, UNITS)
        def _(u):
            g, c = u // CHUNKS, lax.rem(u, CHUNKS)
            for level in range(3):
                for copy in y_copies(level, g, c) + x_copies(level, g, c):
                    copy.wait_send()

        for level in range(3):
            for g in range(GROUPS):
                for up in (False, True):
                    z_copy(level, g, up).wait_send()

    hear(3)
    moved = pltpu.roll(part[...] * F32(1.0 / CELLS), 0, 1, stride=NORB, stride_axis=0)
    pair[0] = jnp.sum(moved.reshape(2, SUB, LX), axis=1)
    to_core = remote(pair.at[0], pair.at[1], gsend.at[0], grecv.at[0], "gz", 1 - 2 * core)
    to_core.start()
    wait_sends()
    to_core.wait_recv()
    mine = (here["gx"] * sizes["gy"] + here["gy"]) * layers + here["gz"] // 2
    seen[mine] = pair[0] + pair[1]
    offsets = [
        (dx, dy, dz)
        for dx in range(sizes["gx"])
        for dy in range(sizes["gy"])
        for dz in range(layers)
    ][1:]
    ring = {"gx": sizes["gx"], "gy": sizes["gy"], "gz": layers}

    def hops(offset):
        return sum(min(d, n - d) for d, n in zip(offset, ring.values()))

    along = {axis: [at(axis, d * (2 if axis == "gz" else 1)) for d in range(ring[axis])] for axis in AXES}
    for offset in sorted(offsets, key=hops, reverse=True):
        pltpu.make_async_remote_copy(
            src_ref=seen.at[mine], dst_ref=seen.at[mine], send_sem=gsend.at[1],
            recv_sem=grecv.at[1],
            device_id={axis: along[axis][d] for axis, d in zip(AXES, offset)},
            device_id_type=MESH,
        ).start()
    others = seen.at[pl.ds(0, len(offsets))]
    pltpu.make_async_copy(others, others, grecv.at[1]).wait()
    terms = [seen[k] for k in range(len(offsets) + 1)]
    while len(terms) > 1:
        terms = [a + b for a, b in zip(terms[::2], terms[1::2])]
    value = terms[0]
    gram_ref[...] = value
    to_core.wait_send()
    pltpu.make_async_copy(others, others, gsend.at[1]).wait()


def solve_kernel(filt, gram_ref, out_hbm, factor_ref, out, out_sem):
    def entry(i, j):
        at = NORB * (i % SUB) + j
        return jnp.broadcast_to(gram_ref[i // SUB : i // SUB + 1, at : at + 1], (SUB, LX))

    row = lax.broadcasted_iota(jnp.int32, (SUB, LX), 0)
    lane = lax.broadcasted_iota(jnp.int32, (SUB, LX), 1)
    lower, inverse = {}, []
    for j in range(NORB):
        column = {i: entry(i, j) for i in range(j, NORB)}
        for k in range(j):
            for i in range(j, NORB):
                column[i] = column[i] - lower[i, k] * lower[j, k]
        root = jnp.sqrt(column[j])
        scale = F32(1) / root
        lower[j, j] = root
        for i in range(j + 1, NORB):
            lower[i, j] = column[i] * scale
        line = jnp.where(lane == j, F32(1), F32(0))
        for m in range(j):
            line = line - lower[j, m] * inverse[m]
        inverse.append(line * scale)

    def stack(lines):
        halves = []
        for half in range(GROUPS):
            rows = lines[half * SUB]
            for i in range(1, SUB):
                rows = jnp.where(row == i, lines[half * SUB + i], rows)
            halves.append(rows)
        return jnp.concatenate(halves, axis=0)

    def gather(entries):
        lines = []
        for i in range(NORB):
            line = jnp.zeros((SUB, LX), F32)
            for j in range(NORB):
                if (i, j) in entries:
                    line = jnp.where(lane == j, entries[i, j], line)
            lines.append(line)
        return stack(lines)

    high, low = split(stack(inverse)[:, :NORB])
    lhs = jnp.concatenate([high, high, low], axis=1)

    def out_copy(c):
        part = pl.ds(c * STEP * LY, STEP * LY)
        return pltpu.make_async_copy(out.at[:, part], out_hbm.at[:, part], out_sem.at[c])

    for c in range(LZ // STEP):
        for z in range(c * STEP, (c + 1) * STEP):
            wide = jnp.concatenate(
                [
                    jnp.concatenate([filt[g, z, y] for g in range(GROUPS)], axis=0)
                    for y in range(LY)
                ],
                axis=1,
            )
            high, low = split(wide)
            solved = jnp.dot(
                lhs, jnp.concatenate([high, low, high], axis=0), preferred_element_type=F32
            )
            for g in range(GROUPS):
                for start in range(0, LY, SUB):
                    block = jnp.stack(
                        [
                            solved[g * SUB : (g + 1) * SUB, y * LX : (y + 1) * LX]
                            for y in range(start, start + SUB)
                        ]
                    )
                    out[pl.ds(g * SUB, SUB), pl.ds(z * LY + start, SUB), :] = jnp.swapaxes(
                        block, 0, 1
                    )
        out_copy(c).start()
    factor_ref[...] = gather({(j, i): value for (i, j), value in lower.items()})[:, :NORB]
    for c in range(LZ // STEP):
        out_copy(c).wait()


def on_device(orbitals, potential):
    hbm = pl.BlockSpec(memory_space=pltpu.HBM)
    vmem = pl.BlockSpec(memory_space=pltpu.VMEM)
    dma = pltpu.SemaphoreType.DMA
    sizes = {axis: lax.axis_size(axis) for axis in AXES}
    filtered, gram = pl.pallas_call(
        filter_kernel,
        name="filter_and_gram",
        out_shape=[
            jax.ShapeDtypeStruct((GROUPS, LZ, LY, SUB, LX), F32),
            jax.ShapeDtypeStruct((2, LX), F32),
        ],
        in_specs=[hbm] * 3,
        out_specs=[vmem, vmem],
        scratch_shapes=[
            pltpu.VMEM((NORB, ROWS, LX), F32),
            *[pltpu.VMEM((GROUPS, LZ + 2 * HALO, LY + 2 * HALO, SUB, LX), F32)] * 3,
            *[pltpu.VMEM((GROUPS, LZ, SUB, LX), F32)] * 3,
            *[pltpu.VMEM((3, GROUPS, LZ, SUB, LX), F32)] * 2,
            pltpu.VMEM((LZ, LY, LX), F32),
            pltpu.VMEM((4 * LX, LX), BF16),
            pltpu.VMEM((NORB, LX), F32),
            pltpu.VMEM((2, 2, LX), F32),
            pltpu.VMEM((sizes["gx"] * sizes["gy"] * sizes["gz"] // 2, 2, LX), F32),
            pltpu.SemaphoreType.REGULAR((4,)),
            dma((UNITS,)),
            dma((2,)),
            dma((3, UNITS, 2)),
            dma((3, UNITS, 2)),
            dma((3, UNITS, 2)),
            dma((3, UNITS, 2)),
            dma((3, GROUPS, 2)),
            dma((3, GROUPS, 2)),
            dma((2,)),
            dma((2,)),
        ],
        compiler_params=pltpu.CompilerParams(
            collective_id=0, has_side_effects=True, vmem_limit_bytes=40 * 2**20
        ),
        cost_estimate=pl.CostEstimate(
            flops=10**9, bytes_accessed=5 * 2**20, transcendentals=0
        ),
    )(*[
        pltpu.with_memory_space_constraint(value, pltpu.HBM)
        for value in (
            orbitals.reshape(NORB, ROWS, LX), potential, jnp.asarray(x_weights())
        )
    ])
    solved, factor = pl.pallas_call(
        solve_kernel,
        name="solve",
        out_shape=[
            jax.ShapeDtypeStruct((NORB, ROWS, LX), F32),
            jax.ShapeDtypeStruct((NORB, NORB), F32),
        ],
        in_specs=[vmem, vmem],
        out_specs=[hbm, vmem],
        scratch_shapes=[
            pltpu.VMEM((NORB, ROWS, LX), F32),
            dma((LZ // STEP,)),
        ],
        compiler_params=pltpu.CompilerParams(vmem_limit_bytes=24 * 2**20),
        cost_estimate=pl.CostEstimate(
            flops=10**8, bytes_accessed=4 * 2**20, transcendentals=0
        ),
    )(filtered, gram)
    return solved.reshape(NORB, LZ, LY, LX), factor


def solution(mesh):
    in_specs = (P(None, "gz", "gy", "gx"), P("gz", "gy", "gx"))
    out_specs = (P(None, "gz", "gy", "gx"), P())
    return jax.shard_map(
        on_device, mesh=mesh, in_specs=in_specs, out_specs=out_specs, check_vma=False
    )
```

```python
import functools

import jax
import jax.numpy as jnp
import ml_dtypes
import numpy as np
from jax import lax
from jax.experimental import pallas as pl
from jax.experimental.pallas import tpu as pltpu
from jax.sharding import PartitionSpec as P

COEFFS = (-205.0 / 72.0, 8.0 / 5.0, -1.0 / 5.0, 8.0 / 315.0, -1.0 / 560.0)
SCALE = 2.0 * -2.0 / 20.0
TAPS = tuple(SCALE * c for c in COEFFS)

NORB, LZ, LY, LX = 16, 16, 16, 128
HALO = 4
SUB = 8
GROUPS = NORB // SUB
SLABS = 4
CHUNKS = LZ // SLABS
UNITS = GROUPS * CHUNKS
QUAD = 8 * HALO
UNROLL = 4
STEP = 2
ROWS = LZ * LY
CELLS = 4194304
F32, BF16 = jnp.float32, jnp.bfloat16
MESH = pl.DeviceIdType.MESH
AXES = ("gx", "gy", "gz")


def x_weights():
    places = np.concatenate([np.arange(LX), np.arange(-HALO, 0), np.arange(LX, LX + HALO)])
    away = np.abs(places[:, None] - np.arange(LX)[None, :])
    full = np.zeros((LX + 2 * HALO, LX), np.float32)
    for k in range(1, HALO + 1):
        full[away == k] = np.float32(TAPS[k])
    high = full.astype(ml_dtypes.bfloat16)
    low = (full - high.astype(np.float32)).astype(ml_dtypes.bfloat16)
    halo = np.zeros((LX, LX), ml_dtypes.bfloat16)
    for start, part in ((0, high), (QUAD, high), (2 * QUAD, low)):
        halo[start : start + 2 * HALO] = part[LX:]
    return np.concatenate([high[:LX], halo, high[:LX], low[:LX]], axis=0)


def split(value):
    high = value.astype(BF16)
    return high, (value - high.astype(F32)).astype(BF16)


def filter_kernel(
    orb_hbm, pot_hbm, w_hbm, last, gram_ref,
    load, buf0, buf1, buf2, pack0, pack1, pack2, from_left, from_right, pv, w_ref, part, pair, seen, word,
    load_sem, small_sem, ysend, yrecv, xsend, xrecv, zsend, zrecv, gsend, grecv,
):
    bufs, packs = (buf0, buf1, buf2), (pack0, pack1, pack2)
    sizes = {axis: lax.axis_size(axis) for axis in AXES}
    here = {axis: lax.axis_index(axis) for axis in AXES}

    def at(axis, step):
        return {axis: lax.rem(here[axis] + (step + sizes[axis]), sizes[axis])}

    neighbours = [(axis, step) for axis in ("gy", "gz", "gx") for step in (1, -1)]
    barrier = pltpu.get_barrier_semaphore()
    for axis, step in neighbours:
        pl.semaphore_signal(barrier, inc=1, device_id=at(axis, step), device_id_type=MESH)

    def load_copy(g, c):
        part = (pl.ds(g * SUB, SUB), pl.ds(c * SLABS * LY, SLABS * LY))
        return pltpu.make_async_copy(
            orb_hbm.at[part], load.at[part], load_sem.at[g * CHUNKS + c]
        )

    small = [
        pltpu.make_async_copy(pot_hbm, pv, small_sem.at[0]),
        pltpu.make_async_copy(w_hbm, w_ref, small_sem.at[1]),
    ]
    for g in range(GROUPS):
        for c in range(CHUNKS):
            load_copy(g, c).start()
    for copy in small:
        copy.start()

    def remote(src, dst, send_sem, recv_sem, axis, step):
        return pltpu.make_async_remote_copy(
            src_ref=src, dst_ref=dst, send_sem=send_sem, recv_sem=recv_sem,
            device_id=at(axis, step), device_id_type=MESH,
        )

    def y_copies(level, g, c):
        u, zs = g * CHUNKS + c, pl.ds(HALO + c * SLABS, SLABS)
        level_buf = bufs[level].at[g, zs]
        return [
            remote(
                level_buf.at[:, pl.ds(LY, HALO)], level_buf.at[:, pl.ds(0, HALO)],
                ysend.at[level, u, 0], yrecv.at[level, u, 0], "gy", 1,
            ),
            remote(
                level_buf.at[:, pl.ds(HALO, HALO)], level_buf.at[:, pl.ds(HALO + LY, HALO)],
                ysend.at[level, u, 1], yrecv.at[level, u, 1], "gy", -1,
            ),
        ]

    def x_copies(level, g, c):
        u, zs = g * CHUNKS + c, pl.ds(c * SLABS, SLABS)
        return [
            remote(
                packs[level].at[g, zs], from_left.at[level, g, zs],
                xsend.at[level, u, 0], xrecv.at[level, u, 0], "gx", 1,
            ),
            remote(
                packs[level].at[g, zs], from_right.at[level, g, zs],
                xsend.at[level, u, 1], xrecv.at[level, u, 1], "gx", -1,
            ),
        ]

    def z_copy(level, g, up):
        inner = pl.ds(HALO, LY)
        src, dst = (LZ, 0) if up else (HALO, HALO + LZ)
        i = 0 if up else 1
        return remote(
            bufs[level].at[g, pl.ds(src, HALO), inner],
            bufs[level].at[g, pl.ds(dst, HALO), inner],
            zsend.at[level, g, i], zrecv.at[level, g, i], "gz", 1 if up else -1,
        )

    def send(level, g, c):
        for copy in y_copies(level, g, c):
            copy.start()

        @pl.when(c == 0)
        def _():
            z_copy(level, g, False).start()

        @pl.when(c == CHUNKS - 1)
        def _():
            z_copy(level, g, True).start()

        for copy in x_copies(level, g, c):
            copy.start()

    lane = lax.broadcasted_iota(jnp.int32, (SUB, LX), 1)

    def pack_edges(values):
        packed = jnp.zeros((SUB, LX), F32)
        for y in range(LY):
            moved = pltpu.roll(values[y], 2 * HALO * y + HALO, 1)
            mine = (lane >= 2 * HALO * y) & (lane < 2 * HALO * (y + 1))
            packed = jnp.where(mine, moved, packed)
        return packed

    flat = load.reshape(NORB * ROWS, LX)

    def start_unit(g, c):
        load_copy(g, c).wait()

        @pl.loop(0, SLABS, unroll=UNROLL)
        def _(s):
            z = c * SLABS + s
            values = []
            for y in range(LY):
                v = flat[pl.ds(g * SUB * ROWS + z * LY + y, SUB, stride=ROWS), :]
                buf0[g, HALO + z, HALO + y] = v
                values.append(v)
            pack0[g, z] = pack_edges(values)

    start_unit(0, 0)
    pl.semaphore_wait(barrier, len(neighbours))
    send(0, 0, 0)

    @pl.loop(1, UNITS)
    def _(u):
        g, c = u // CHUNKS, lax.rem(u, CHUNKS)
        start_unit(g, c)
        send(0, g, c)

    for copy in small:
        copy.wait()
    pv[...] = pv[...] * F32(0.1) + F32(3.0 * TAPS[0] - 2.3)

    def stencil(level, g, z):
        buf = bufs[level]
        edges = jnp.where(
            lax.rem(lane, 2 * HALO) < HALO, from_left[level, g, z], from_right[level, g, z]
        )
        edge_high = edges.astype(BF16).astype(F32)
        parts = (
            edge_high,
            pltpu.roll(edges - edge_high, QUAD, 1),
            pltpu.roll(edge_high, 2 * QUAD, 1),
        )
        halo = []
        for quad in range(LX // QUAD):
            own = parts[2]
            for i in (1, 0):
                own = jnp.where(lane // QUAD == (quad + i) % (LX // QUAD), parts[i], own)
            for y in range(QUAD // 8 * quad, QUAD // 8 * (quad + 1)):
                halo.append(pltpu.roll(own, (LX - 2 * HALO * y) % LX, 1))
        centre = [buf[g, HALO + z, HALO + y] for y in range(LY)]
        high, low = split(jnp.concatenate(centre, axis=0))
        rows = jnp.concatenate(
            [high, jnp.concatenate(halo, axis=0).astype(BF16), low, high], axis=1
        )
        along_x = jnp.dot(rows, w_ref[...], preferred_element_type=F32)
        out = []
        for y in range(LY):
            total = pv[z, pl.ds(y, 1), :] * centre[y] + along_x[y * SUB : (y + 1) * SUB]
            for k in range(1, HALO + 1):
                around = (
                    buf[g, HALO + z + k, HALO + y] + buf[g, HALO + z - k, HALO + y]
                ) + (buf[g, HALO + z, HALO + y + k] + buf[g, HALO + z, HALO + y - k])
                total = total + F32(TAPS[k]) * around
            out.append(total)
        return out

    def wait_halos(level, g, c):
        for copy in y_copies(level, g, c) + x_copies(level, g, c):
            copy.wait_recv()

        @pl.when(c == 0)
        def _():
            z_copy(level, g, True).wait_recv()

        @pl.when(c == CHUNKS - 1)
        def _():
            z_copy(level, g, False).wait_recv()

    core = lax.rem(here["gz"], 2)
    layers = sizes["gz"] // 2
    rounds = (
        [("gx", d) for d in range(1, sizes["gx"])],
        [("gy", d) for d in range(1, sizes["gy"])],
        [("gz", 2), ("gz", -2)],
        [("gz", d) for d in range(4, sizes["gz"] - 3, 2)],
    )

    def tell(i):
        for axis, step in rounds[i]:
            pl.semaphore_signal(
                word.at[i], inc=1, device_id=at(axis, step), device_id_type=MESH
            )

    def hear(i):
        pl.semaphore_wait(word.at[i], len(rounds[i]))

    for level in (1, 2):
        if level == 2:
            tell(0)

        @pl.loop(0, UNITS)
        def _(u, level=level):
            g, c = u // CHUNKS, lax.rem(u, CHUNKS)
            wait_halos(level - 1, g, c)

            if level == 2:

                @pl.when(u == CHUNKS)
                def _():
                    hear(0)
                    tell(1)

            @pl.loop(0, SLABS, unroll=UNROLL)
            def _(s):
                z = c * SLABS + s
                new = stencil(level - 1, g, z)
                if level == 1:
                    new = [F32(0.5) * v for v in new]
                else:
                    new = [v - buf0[g, HALO + z, HALO + y] for y, v in enumerate(new)]
                for y in range(LY):
                    bufs[level][g, HALO + z, HALO + y] = new[y]
                packs[level][g, z] = pack_edges(new)

            send(level, g, c)

    hear(1)
    tell(2)
    part[...] = jnp.zeros_like(part)

    @pl.loop(0, UNITS)
    def _(u):
        g, c = u // CHUNKS, lax.rem(u, CHUNKS)
        wait_halos(2, g, c)

        @pl.when(u == CHUNKS)
        def _():
            hear(2)
            tell(3)

        @pl.loop(0, SLABS, unroll=UNROLL)
        def _(s):
            z = c * SLABS + s
            new = stencil(2, g, z)
            for y in range(LY):
                last[g, z, y] = new[y] - buf1[g, HALO + z, HALO + y]

        @pl.when(g == GROUPS - 1)
        def _():
            @pl.loop(0, SLABS, unroll=UNROLL)
            def _(s):
                z = c * SLABS + s
                wide = jnp.concatenate(
                    [
                        jnp.concatenate([last[k, z, y] for k in range(GROUPS)], axis=0)
                        for y in range(LY)
                    ],
                    axis=1,
                )
                high, low = split(wide)
                both = jnp.concatenate([high, low], axis=0)
                quad = lax.dot_general(
                    both, both, (((1,), (1,)), ((), ())), preferred_element_type=F32
                )
                four = quad[:NORB] + quad[NORB:]
                part[:, :NORB] += four[:, :NORB] + four[:, NORB:]

    def wait_sends():
        @pl.loop(0, UNITS)
        def _(u):
            g, c = u // CHUNKS, lax.rem(u, CHUNKS)
            for level in range(3):
                for copy in y_copies(level, g, c) + x_copies(level, g, c):
                    copy.wait_send()

        for level in range(3):
            for g in range(GROUPS):
                for up in (False, True):
                    z_copy(level, g, up).wait_send()

    hear(3)
    moved = pltpu.roll(part[...] * F32(1.0 / CELLS), 0, 1, stride=NORB, stride_axis=0)
    pair[0] = jnp.sum(moved.reshape(2, SUB, LX), axis=1)
    to_core = remote(pair.at[0], pair.at[1], gsend.at[0], grecv.at[0], "gz", 1 - 2 * core)
    to_core.start()
    wait_sends()
    to_core.wait_recv()
    mine = (here["gx"] * sizes["gy"] + here["gy"]) * layers + here["gz"] // 2
    seen[mine] = pair[0] + pair[1]
    offsets = [
        (dx, dy, dz)
        for dx in range(sizes["gx"])
        for dy in range(sizes["gy"])
        for dz in range(layers)
    ][1:]
    ring = {"gx": sizes["gx"], "gy": sizes["gy"], "gz": layers}

    def hops(offset):
        return sum(min(d, n - d) for d, n in zip(offset, ring.values()))

    along = {axis: [at(axis, d * (2 if axis == "gz" else 1)) for d in range(ring[axis])] for axis in AXES}
    for offset in sorted(offsets, key=hops, reverse=True):
        pltpu.make_async_remote_copy(
            src_ref=seen.at[mine], dst_ref=seen.at[mine], send_sem=gsend.at[1],
            recv_sem=grecv.at[1],
            device_id={axis: along[axis][d] for axis, d in zip(AXES, offset)},
            device_id_type=MESH,
        ).start()
    others = seen.at[pl.ds(0, len(offsets))]
    pltpu.make_async_copy(others, others, grecv.at[1]).wait()
    terms = [seen[k] for k in range(len(offsets) + 1)]
    while len(terms) > 1:
        terms = [a + b for a, b in zip(terms[::2], terms[1::2])]
    value = terms[0]
    gram_ref[...] = value
    to_core.wait_send()
    pltpu.make_async_copy(others, others, gsend.at[1]).wait()


def solve_kernel(filt, gram_ref, out_hbm, factor_hbm, out, factor_ref, out_sem, factor_sem):
    def entry(i, j):
        at = NORB * (i % SUB) + j
        return jnp.broadcast_to(gram_ref[i // SUB : i // SUB + 1, at : at + 1], (SUB, LX))

    row = lax.broadcasted_iota(jnp.int32, (SUB, LX), 0)
    lane = lax.broadcasted_iota(jnp.int32, (SUB, LX), 1)
    lower, inverse = {}, []
    for j in range(NORB):
        column = {i: entry(i, j) for i in range(j, NORB)}
        for k in range(j):
            for i in range(j, NORB):
                column[i] = column[i] - lower[i, k] * lower[j, k]
        root = jnp.sqrt(column[j])
        scale = F32(1) / root
        lower[j, j] = root
        for i in range(j + 1, NORB):
            lower[i, j] = column[i] * scale
        line = jnp.where(lane == j, F32(1), F32(0))
        for m in range(j):
            line = line - lower[j, m] * inverse[m]
        inverse.append(line * scale)

    def stack(lines):
        halves = []
        for half in range(GROUPS):
            rows = lines[half * SUB]
            for i in range(1, SUB):
                rows = jnp.where(row == i, lines[half * SUB + i], rows)
            halves.append(rows)
        return jnp.concatenate(halves, axis=0)

    def gather(entries):
        lines = []
        for i in range(NORB):
            line = jnp.zeros((SUB, LX), F32)
            for j in range(NORB):
                if (i, j) in entries:
                    line = jnp.where(lane == j, entries[i, j], line)
            lines.append(line)
        return stack(lines)

    high, low = split(stack(inverse)[:, :NORB])
    lhs = jnp.concatenate([high, high, low], axis=1)

    factor_ref[...] = gather({(j, i): value for (i, j), value in lower.items()})[:, :NORB]
    factor_copy = pltpu.make_async_copy(factor_ref, factor_hbm, factor_sem)

    def out_copy(c):
        part = pl.ds(c * STEP * LY, STEP * LY)
        return pltpu.make_async_copy(out.at[:, part], out_hbm.at[:, part], out_sem.at[c])

    for c in range(LZ // STEP):
        for z in range(c * STEP, (c + 1) * STEP):
            wide = jnp.concatenate(
                [
                    jnp.concatenate([filt[g, z, y] for g in range(GROUPS)], axis=0)
                    for y in range(LY)
                ],
                axis=1,
            )
            high, low = split(wide)
            solved = jnp.dot(
                lhs, jnp.concatenate([high, low, high], axis=0), preferred_element_type=F32
            )
            for g in range(GROUPS):
                for start in range(0, LY, SUB):
                    block = jnp.stack(
                        [
                            solved[g * SUB : (g + 1) * SUB, y * LX : (y + 1) * LX]
                            for y in range(start, start + SUB)
                        ]
                    )
                    out[pl.ds(g * SUB, SUB), pl.ds(z * LY + start, SUB), :] = jnp.swapaxes(
                        block, 0, 1
                    )
        out_copy(c).start()
        if c == 0:
            factor_copy.start()
    factor_copy.wait()
    for c in range(LZ // STEP):
        out_copy(c).wait()


def on_device(orbitals, potential):
    hbm = pl.BlockSpec(memory_space=pltpu.HBM)
    vmem = pl.BlockSpec(memory_space=pltpu.VMEM)
    dma = pltpu.SemaphoreType.DMA
    sizes = {axis: lax.axis_size(axis) for axis in AXES}
    filtered, gram = pl.pallas_call(
        filter_kernel,
        name="filter_and_gram",
        out_shape=[
            jax.ShapeDtypeStruct((GROUPS, LZ, LY, SUB, LX), F32),
            jax.ShapeDtypeStruct((2, LX), F32),
        ],
        in_specs=[hbm] * 3,
        out_specs=[vmem, vmem],
        scratch_shapes=[
            pltpu.VMEM((NORB, ROWS, LX), F32),
            *[pltpu.VMEM((GROUPS, LZ + 2 * HALO, LY + 2 * HALO, SUB, LX), F32)] * 3,
            *[pltpu.VMEM((GROUPS, LZ, SUB, LX), F32)] * 3,
            *[pltpu.VMEM((3, GROUPS, LZ, SUB, LX), F32)] * 2,
            pltpu.VMEM((LZ, LY, LX), F32),
            pltpu.VMEM((4 * LX, LX), BF16),
            pltpu.VMEM((NORB, LX), F32),
            pltpu.VMEM((2, 2, LX), F32),
            pltpu.VMEM((sizes["gx"] * sizes["gy"] * sizes["gz"] // 2, 2, LX), F32),
            pltpu.SemaphoreType.REGULAR((4,)),
            dma((UNITS,)),
            dma((2,)),
            dma((3, UNITS, 2)),
            dma((3, UNITS, 2)),
            dma((3, UNITS, 2)),
            dma((3, UNITS, 2)),
            dma((3, GROUPS, 2)),
            dma((3, GROUPS, 2)),
            dma((2,)),
            dma((2,)),
        ],
        compiler_params=pltpu.CompilerParams(
            collective_id=0, has_side_effects=True, vmem_limit_bytes=40 * 2**20
        ),
        cost_estimate=pl.CostEstimate(
            flops=10**9, bytes_accessed=5 * 2**20, transcendentals=0
        ),
    )(*[
        pltpu.with_memory_space_constraint(value, pltpu.HBM)
        for value in (
            orbitals.reshape(NORB, ROWS, LX), potential, jnp.asarray(x_weights())
        )
    ])
    solved, factor = pl.pallas_call(
        solve_kernel,
        name="solve",
        out_shape=[
            jax.ShapeDtypeStruct((NORB, ROWS, LX), F32),
            jax.ShapeDtypeStruct((NORB, NORB), F32),
        ],
        in_specs=[vmem, vmem],
        out_specs=[hbm, hbm],
        scratch_shapes=[
            pltpu.VMEM((NORB, ROWS, LX), F32),
            pltpu.VMEM((NORB, NORB), F32),
            dma((LZ // STEP,)),
            dma(()),
        ],
        compiler_params=pltpu.CompilerParams(vmem_limit_bytes=24 * 2**20),
        cost_estimate=pl.CostEstimate(
            flops=10**8, bytes_accessed=4 * 2**20, transcendentals=0
        ),
    )(filtered, gram)
    return solved.reshape(NORB, LZ, LY, LX), factor


def solution(mesh):
    in_specs = (P(None, "gz", "gy", "gx"), P("gz", "gy", "gx"))
    out_specs = (P(None, "gz", "gy", "gx"), P())
    return jax.shard_map(
        on_device, mesh=mesh, in_specs=in_specs, out_specs=out_specs, check_vma=False
    )
```

```python
import functools

import jax
import jax.numpy as jnp
import ml_dtypes
import numpy as np
from jax import lax
from jax.experimental import pallas as pl
from jax.experimental.pallas import tpu as pltpu
from jax.sharding import PartitionSpec as P

COEFFS = (-205.0 / 72.0, 8.0 / 5.0, -1.0 / 5.0, 8.0 / 315.0, -1.0 / 560.0)
SCALE = 2.0 * -2.0 / 20.0
TAPS = tuple(SCALE * c for c in COEFFS)

NORB, LZ, LY, LX = 16, 16, 16, 128
HALO = 4
SUB = 8
GROUPS = NORB // SUB
SLABS = 4
CHUNKS = LZ // SLABS
UNITS = GROUPS * CHUNKS
QUAD = 8 * HALO
UNROLL = 4
STEP = 2
ROWS = LZ * LY
CELLS = 4194304
F32, BF16 = jnp.float32, jnp.bfloat16
MESH = pl.DeviceIdType.MESH
AXES = ("gx", "gy", "gz")


def x_weights():
    places = np.concatenate([np.arange(LX), np.arange(-HALO, 0), np.arange(LX, LX + HALO)])
    away = np.abs(places[:, None] - np.arange(LX)[None, :])
    full = np.zeros((LX + 2 * HALO, LX), np.float32)
    for k in range(1, HALO + 1):
        full[away == k] = np.float32(TAPS[k])
    high = full.astype(ml_dtypes.bfloat16)
    low = (full - high.astype(np.float32)).astype(ml_dtypes.bfloat16)
    halo = np.zeros((LX, LX), ml_dtypes.bfloat16)
    for start, part in ((0, high), (QUAD, high), (2 * QUAD, low)):
        halo[start : start + 2 * HALO] = part[LX:]
    return np.concatenate([high[:LX], halo, high[:LX], low[:LX]], axis=0)


def split(value):
    high = value.astype(BF16)
    return high, (value - high.astype(F32)).astype(BF16)


def filter_kernel(
    orb_hbm, pot_hbm, w_hbm, last, gram_ref,
    load, buf0, buf1, buf2, pack0, pack1, pack2, from_left, from_right, pv, w_ref, part, pair, seen, word,
    load_sem, small_sem, ysend, yrecv, xsend, xrecv, zsend, zrecv, gsend, grecv,
):
    bufs, packs = (buf0, buf1, buf2), (pack0, pack1, pack2)
    sizes = {axis: lax.axis_size(axis) for axis in AXES}
    here = {axis: lax.axis_index(axis) for axis in AXES}

    def at(axis, step):
        return {axis: lax.rem(here[axis] + (step + sizes[axis]), sizes[axis])}

    neighbours = [(axis, step) for axis in ("gy", "gz", "gx") for step in (1, -1)]
    barrier = pltpu.get_barrier_semaphore()
    for axis, step in neighbours:
        pl.semaphore_signal(barrier, inc=1, device_id=at(axis, step), device_id_type=MESH)

    def load_copy(g, c):
        part = (pl.ds(g * SUB, SUB), pl.ds(c * SLABS * LY, SLABS * LY))
        return pltpu.make_async_copy(
            orb_hbm.at[part], load.at[part], load_sem.at[g * CHUNKS + c]
        )

    small = [
        pltpu.make_async_copy(pot_hbm, pv, small_sem.at[0]),
        pltpu.make_async_copy(w_hbm, w_ref, small_sem.at[1]),
    ]
    for g in range(GROUPS):
        for c in range(CHUNKS):
            load_copy(g, c).start()
    for copy in small:
        copy.start()

    def remote(src, dst, send_sem, recv_sem, axis, step):
        return pltpu.make_async_remote_copy(
            src_ref=src, dst_ref=dst, send_sem=send_sem, recv_sem=recv_sem,
            device_id=at(axis, step), device_id_type=MESH,
        )

    def y_copies(level, g, c):
        u, zs = g * CHUNKS + c, pl.ds(HALO + c * SLABS, SLABS)
        level_buf = bufs[level].at[g, zs]
        return [
            remote(
                level_buf.at[:, pl.ds(LY, HALO)], level_buf.at[:, pl.ds(0, HALO)],
                ysend.at[level, u, 0], yrecv.at[level, u, 0], "gy", 1,
            ),
            remote(
                level_buf.at[:, pl.ds(HALO, HALO)], level_buf.at[:, pl.ds(HALO + LY, HALO)],
                ysend.at[level, u, 1], yrecv.at[level, u, 1], "gy", -1,
            ),
        ]

    def x_copies(level, g, c):
        u, zs = g * CHUNKS + c, pl.ds(c * SLABS, SLABS)
        return [
            remote(
                packs[level].at[g, zs], from_left.at[level, g, zs],
                xsend.at[level, u, 0], xrecv.at[level, u, 0], "gx", 1,
            ),
            remote(
                packs[level].at[g, zs], from_right.at[level, g, zs],
                xsend.at[level, u, 1], xrecv.at[level, u, 1], "gx", -1,
            ),
        ]

    def z_copy(level, g, up):
        inner = pl.ds(HALO, LY)
        src, dst = (LZ, 0) if up else (HALO, HALO + LZ)
        i = 0 if up else 1
        return remote(
            bufs[level].at[g, pl.ds(src, HALO), inner],
            bufs[level].at[g, pl.ds(dst, HALO), inner],
            zsend.at[level, g, i], zrecv.at[level, g, i], "gz", 1 if up else -1,
        )

    def send(level, g, c):
        for copy in y_copies(level, g, c):
            copy.start()

        @pl.when(c == 0)
        def _():
            z_copy(level, g, False).start()

        @pl.when(c == CHUNKS - 1)
        def _():
            z_copy(level, g, True).start()

        for copy in x_copies(level, g, c):
            copy.start()

    lane = lax.broadcasted_iota(jnp.int32, (SUB, LX), 1)

    def pack_edges(values):
        packed = jnp.zeros((SUB, LX), F32)
        for y in range(LY):
            moved = pltpu.roll(values[y], 2 * HALO * y + HALO, 1)
            mine = (lane >= 2 * HALO * y) & (lane < 2 * HALO * (y + 1))
            packed = jnp.where(mine, moved, packed)
        return packed

    flat = load.reshape(NORB * ROWS, LX)

    def start_unit(g, c):
        load_copy(g, c).wait()

        @pl.loop(0, SLABS, unroll=UNROLL)
        def _(s):
            z = c * SLABS + s
            values = []
            for y in range(LY):
                v = flat[pl.ds(g * SUB * ROWS + z * LY + y, SUB, stride=ROWS), :]
                buf0[g, HALO + z, HALO + y] = v
                values.append(v)
            pack0[g, z] = pack_edges(values)

    start_unit(0, 0)
    pl.semaphore_wait(barrier, len(neighbours))
    send(0, 0, 0)

    @pl.loop(1, UNITS)
    def _(u):
        g, c = u // CHUNKS, lax.rem(u, CHUNKS)
        start_unit(g, c)
        send(0, g, c)

    for copy in small:
        copy.wait()
    pv[...] = pv[...] * F32(0.1) + F32(3.0 * TAPS[0] - 2.3)

    def stencil(level, g, z, y_halo=True):
        buf = bufs[level]
        edges = jnp.where(
            lax.rem(lane, 2 * HALO) < HALO, from_left[level, g, z], from_right[level, g, z]
        )
        edge_high = edges.astype(BF16).astype(F32)
        parts = (
            edge_high,
            pltpu.roll(edges - edge_high, QUAD, 1),
            pltpu.roll(edge_high, 2 * QUAD, 1),
        )
        halo = []
        for quad in range(LX // QUAD):
            own = parts[2]
            for i in (1, 0):
                own = jnp.where(lane // QUAD == (quad + i) % (LX // QUAD), parts[i], own)
            for y in range(QUAD // 8 * quad, QUAD // 8 * (quad + 1)):
                halo.append(pltpu.roll(own, (LX - 2 * HALO * y) % LX, 1))
        centre = [buf[g, HALO + z, HALO + y] for y in range(LY)]
        high, low = split(jnp.concatenate(centre, axis=0))
        rows = jnp.concatenate(
            [high, jnp.concatenate(halo, axis=0).astype(BF16), low, high], axis=1
        )
        along_x = jnp.dot(rows, w_ref[...], preferred_element_type=F32)
        out = []
        for y in range(LY):
            total = pv[z, pl.ds(y, 1), :] * centre[y] + along_x[y * SUB : (y + 1) * SUB]
            for k in range(1, HALO + 1):
                around = buf[g, HALO + z + k, HALO + y] + buf[g, HALO + z - k, HALO + y]
                rows_k = [r for r in (y + k, y - k) if y_halo or 0 <= r < LY]
                if rows_k:
                    beside = buf[g, HALO + z, HALO + rows_k[0]]
                    for r in rows_k[1:]:
                        beside = beside + buf[g, HALO + z, HALO + r]
                    around = around + beside
                total = total + F32(TAPS[k]) * around
            out.append(total)
        return out

    def wait_y(level, g, c):
        for copy in y_copies(level, g, c):
            copy.wait_recv()

    def wait_xz(level, g, c):
        for copy in x_copies(level, g, c):
            copy.wait_recv()

        @pl.when(c == 0)
        def _():
            z_copy(level, g, True).wait_recv()

        @pl.when(c == CHUNKS - 1)
        def _():
            z_copy(level, g, False).wait_recv()

    core = lax.rem(here["gz"], 2)
    layers = sizes["gz"] // 2
    rounds = (
        [("gx", d) for d in range(1, sizes["gx"])],
        [("gy", d) for d in range(1, sizes["gy"])],
        [("gz", 2), ("gz", -2)],
        [("gz", d) for d in range(4, sizes["gz"] - 3, 2)],
    )

    def tell(i):
        for axis, step in rounds[i]:
            pl.semaphore_signal(
                word.at[i], inc=1, device_id=at(axis, step), device_id_type=MESH
            )

    def hear(i):
        pl.semaphore_wait(word.at[i], len(rounds[i]))

    for level in (1, 2):
        if level == 2:
            tell(0)

        @pl.loop(0, UNITS)
        def _(u, level=level):
            g, c = u // CHUNKS, lax.rem(u, CHUNKS)
            wait_y(level - 1, g, c)
            wait_xz(level - 1, g, c)

            if level == 2:

                @pl.when(u == CHUNKS)
                def _():
                    hear(0)
                    tell(1)

            @pl.loop(0, SLABS, unroll=UNROLL)
            def _(s):
                z = c * SLABS + s
                new = stencil(level - 1, g, z)
                if level == 1:
                    new = [F32(0.5) * v for v in new]
                else:
                    new = [v - buf0[g, HALO + z, HALO + y] for y, v in enumerate(new)]
                for y in range(LY):
                    bufs[level][g, HALO + z, HALO + y] = new[y]
                packs[level][g, z] = pack_edges(new)

            send(level, g, c)

    hear(1)
    tell(2)
    part[...] = jnp.zeros_like(part)

    def add_gram(g, zs, ys):
        @pl.when(g == GROUPS - 1)
        def _():
            total = jnp.zeros((2 * NORB, 2 * NORB), F32)
            for z in zs:
                wide = jnp.concatenate(
                    [
                        jnp.concatenate([last[k, z, y] for k in range(GROUPS)], axis=0)
                        for y in ys
                    ],
                    axis=1,
                )
                both = jnp.concatenate(split(wide), axis=0)
                total += lax.dot_general(
                    both, both, (((1,), (1,)), ((), ())), preferred_element_type=F32
                )
            four = total[:NORB] + total[NORB:]
            part[:, :NORB] += four[:, :NORB] + four[:, NORB:]

    @pl.loop(0, UNITS)
    def _(u):
        g, c = u // CHUNKS, lax.rem(u, CHUNKS)
        wait_xz(2, g, c)

        @pl.when(u == CHUNKS)
        def _():
            hear(2)
            tell(3)

        zs = [c * SLABS + s for s in range(SLABS)]
        for z in zs:
            new = stencil(2, g, z, y_halo=False)
            for y in range(LY):
                last[g, z, y] = new[y] - buf1[g, HALO + z, HALO + y]
        add_gram(g, zs, range(HALO, LY - HALO))

    @pl.loop(0, UNITS)
    def _(u):
        g, c = u // CHUNKS, lax.rem(u, CHUNKS)
        zs = [c * SLABS + s for s in range(SLABS)]
        wait_y(2, g, c)
        edge = [*range(HALO), *range(LY - HALO, LY)]
        for z in zs:
            for y in edge:
                total = last[g, z, y]
                for k in range(1, HALO + 1):
                    for r in (y + k, y - k):
                        if not 0 <= r < LY:
                            total = total + F32(TAPS[k]) * buf2[g, HALO + z, HALO + r]
                last[g, z, y] = total
        add_gram(g, zs, edge)

    def wait_sends():
        @pl.loop(0, UNITS)
        def _(u):
            g, c = u // CHUNKS, lax.rem(u, CHUNKS)
            for level in range(3):
                for copy in y_copies(level, g, c) + x_copies(level, g, c):
                    copy.wait_send()

        for level in range(3):
            for g in range(GROUPS):
                for up in (False, True):
                    z_copy(level, g, up).wait_send()

    hear(3)
    moved = pltpu.roll(part[...] * F32(1.0 / CELLS), 0, 1, stride=NORB, stride_axis=0)
    pair[0] = jnp.sum(moved.reshape(2, SUB, LX), axis=1)
    to_core = remote(pair.at[0], pair.at[1], gsend.at[0], grecv.at[0], "gz", 1 - 2 * core)
    to_core.start()
    wait_sends()
    to_core.wait_recv()
    mine = (here["gx"] * sizes["gy"] + here["gy"]) * layers + here["gz"] // 2
    seen[mine] = pair[0] + pair[1]
    offsets = [
        (dx, dy, dz)
        for dx in range(sizes["gx"])
        for dy in range(sizes["gy"])
        for dz in range(layers)
    ][1:]
    ring = {"gx": sizes["gx"], "gy": sizes["gy"], "gz": layers}

    def hops(offset):
        return sum(min(d, n - d) for d, n in zip(offset, ring.values()))

    along = {axis: [at(axis, d * (2 if axis == "gz" else 1)) for d in range(ring[axis])] for axis in AXES}
    for offset in sorted(offsets, key=hops, reverse=True):
        pltpu.make_async_remote_copy(
            src_ref=seen.at[mine], dst_ref=seen.at[mine], send_sem=gsend.at[1],
            recv_sem=grecv.at[1],
            device_id={axis: along[axis][d] for axis, d in zip(AXES, offset)},
            device_id_type=MESH,
        ).start()
    others = seen.at[pl.ds(0, len(offsets))]
    pltpu.make_async_copy(others, others, grecv.at[1]).wait()
    terms = [seen[k] for k in range(len(offsets) + 1)]
    while len(terms) > 1:
        terms = [a + b for a, b in zip(terms[::2], terms[1::2])]
    value = terms[0]
    gram_ref[...] = value
    to_core.wait_send()
    pltpu.make_async_copy(others, others, gsend.at[1]).wait()


def solve_kernel(filt, gram_ref, out_hbm, factor_hbm, out, factor_ref, out_sem, factor_sem):
    def entry(i, j):
        at = NORB * (i % SUB) + j
        return jnp.broadcast_to(gram_ref[i // SUB : i // SUB + 1, at : at + 1], (SUB, LX))

    row = lax.broadcasted_iota(jnp.int32, (SUB, LX), 0)
    lane = lax.broadcasted_iota(jnp.int32, (SUB, LX), 1)
    lower, inverse = {}, []
    for j in range(NORB):
        column = {i: entry(i, j) for i in range(j, NORB)}
        for k in range(j):
            for i in range(j, NORB):
                column[i] = column[i] - lower[i, k] * lower[j, k]
        root = jnp.sqrt(column[j])
        scale = F32(1) / root
        lower[j, j] = root
        for i in range(j + 1, NORB):
            lower[i, j] = column[i] * scale
        line = jnp.where(lane == j, F32(1), F32(0))
        for m in range(j):
            line = line - lower[j, m] * inverse[m]
        inverse.append(line * scale)

    def stack(lines):
        halves = []
        for half in range(GROUPS):
            rows = lines[half * SUB]
            for i in range(1, SUB):
                rows = jnp.where(row == i, lines[half * SUB + i], rows)
            halves.append(rows)
        return jnp.concatenate(halves, axis=0)

    def gather(entries):
        lines = []
        for i in range(NORB):
            line = jnp.zeros((SUB, LX), F32)
            for j in range(NORB):
                if (i, j) in entries:
                    line = jnp.where(lane == j, entries[i, j], line)
            lines.append(line)
        return stack(lines)

    high, low = split(stack(inverse)[:, :NORB])
    lhs = jnp.concatenate([high, high, low], axis=1)

    factor_ref[...] = gather({(j, i): value for (i, j), value in lower.items()})[:, :NORB]
    factor_copy = pltpu.make_async_copy(factor_ref, factor_hbm, factor_sem)

    def out_copy(c):
        part = pl.ds(c * STEP * LY, STEP * LY)
        return pltpu.make_async_copy(out.at[:, part], out_hbm.at[:, part], out_sem.at[c])

    for c in range(LZ // STEP):
        for z in range(c * STEP, (c + 1) * STEP):
            wide = jnp.concatenate(
                [
                    jnp.concatenate([filt[g, z, y] for g in range(GROUPS)], axis=0)
                    for y in range(LY)
                ],
                axis=1,
            )
            high, low = split(wide)
            solved = jnp.dot(
                lhs, jnp.concatenate([high, low, high], axis=0), preferred_element_type=F32
            )
            for g in range(GROUPS):
                for start in range(0, LY, SUB):
                    block = jnp.stack(
                        [
                            solved[g * SUB : (g + 1) * SUB, y * LX : (y + 1) * LX]
                            for y in range(start, start + SUB)
                        ]
                    )
                    out[pl.ds(g * SUB, SUB), pl.ds(z * LY + start, SUB), :] = jnp.swapaxes(
                        block, 0, 1
                    )
        out_copy(c).start()
        if c == 0:
            factor_copy.start()
    factor_copy.wait()
    for c in range(LZ // STEP):
        out_copy(c).wait()


def on_device(orbitals, potential):
    hbm = pl.BlockSpec(memory_space=pltpu.HBM)
    vmem = pl.BlockSpec(memory_space=pltpu.VMEM)
    dma = pltpu.SemaphoreType.DMA
    sizes = {axis: lax.axis_size(axis) for axis in AXES}
    filtered, gram = pl.pallas_call(
        filter_kernel,
        name="filter_and_gram",
        out_shape=[
            jax.ShapeDtypeStruct((GROUPS, LZ, LY, SUB, LX), F32),
            jax.ShapeDtypeStruct((2, LX), F32),
        ],
        in_specs=[hbm] * 3,
        out_specs=[vmem, vmem],
        scratch_shapes=[
            pltpu.VMEM((NORB, ROWS, LX), F32),
            *[pltpu.VMEM((GROUPS, LZ + 2 * HALO, LY + 2 * HALO, SUB, LX), F32)] * 3,
            *[pltpu.VMEM((GROUPS, LZ, SUB, LX), F32)] * 3,
            *[pltpu.VMEM((3, GROUPS, LZ, SUB, LX), F32)] * 2,
            pltpu.VMEM((LZ, LY, LX), F32),
            pltpu.VMEM((4 * LX, LX), BF16),
            pltpu.VMEM((NORB, LX), F32),
            pltpu.VMEM((2, 2, LX), F32),
            pltpu.VMEM((sizes["gx"] * sizes["gy"] * sizes["gz"] // 2, 2, LX), F32),
            pltpu.SemaphoreType.REGULAR((4,)),
            dma((UNITS,)),
            dma((2,)),
            dma((3, UNITS, 2)),
            dma((3, UNITS, 2)),
            dma((3, UNITS, 2)),
            dma((3, UNITS, 2)),
            dma((3, GROUPS, 2)),
            dma((3, GROUPS, 2)),
            dma((2,)),
            dma((2,)),
        ],
        compiler_params=pltpu.CompilerParams(
            collective_id=0, has_side_effects=True, vmem_limit_bytes=40 * 2**20
        ),
        cost_estimate=pl.CostEstimate(
            flops=10**9, bytes_accessed=5 * 2**20, transcendentals=0
        ),
    )(*[
        pltpu.with_memory_space_constraint(value, pltpu.HBM)
        for value in (
            orbitals.reshape(NORB, ROWS, LX), potential, jnp.asarray(x_weights())
        )
    ])
    solved, factor = pl.pallas_call(
        solve_kernel,
        name="solve",
        out_shape=[
            jax.ShapeDtypeStruct((NORB, ROWS, LX), F32),
            jax.ShapeDtypeStruct((NORB, NORB), F32),
        ],
        in_specs=[vmem, vmem],
        out_specs=[hbm, hbm],
        scratch_shapes=[
            pltpu.VMEM((NORB, ROWS, LX), F32),
            pltpu.VMEM((NORB, NORB), F32),
            dma((LZ // STEP,)),
            dma(()),
        ],
        compiler_params=pltpu.CompilerParams(vmem_limit_bytes=24 * 2**20),
        cost_estimate=pl.CostEstimate(
            flops=10**8, bytes_accessed=4 * 2**20, transcendentals=0
        ),
    )(filtered, gram)
    return solved.reshape(NORB, LZ, LY, LX), factor


def solution(mesh):
    in_specs = (P(None, "gz", "gy", "gx"), P("gz", "gy", "gx"))
    out_specs = (P(None, "gz", "gy", "gx"), P())
    return jax.shard_map(
        on_device, mesh=mesh, in_specs=in_specs, out_specs=out_specs, check_vma=False
    )
```

```python
import functools

import jax
import jax.numpy as jnp
import ml_dtypes
import numpy as np
from jax import lax
from jax.experimental import pallas as pl
from jax.experimental.pallas import tpu as pltpu
from jax.sharding import PartitionSpec as P

COEFFS = (-205.0 / 72.0, 8.0 / 5.0, -1.0 / 5.0, 8.0 / 315.0, -1.0 / 560.0)
SCALE = 2.0 * -2.0 / 20.0
TAPS = tuple(SCALE * c for c in COEFFS)

NORB, LZ, LY, LX = 16, 16, 16, 128
HALO = 4
SUB = 8
GROUPS = NORB // SUB
SLABS = 4
CHUNKS = LZ // SLABS
UNITS = GROUPS * CHUNKS
QUAD = 8 * HALO
UNROLL = 4
STEP = 2
ROWS = LZ * LY
CELLS = 4194304
F32, BF16 = jnp.float32, jnp.bfloat16
MESH = pl.DeviceIdType.MESH
AXES = ("gx", "gy", "gz")


def x_weights():
    places = np.concatenate([np.arange(LX), np.arange(-HALO, 0), np.arange(LX, LX + HALO)])
    away = np.abs(places[:, None] - np.arange(LX)[None, :])
    full = np.zeros((LX + 2 * HALO, LX), np.float32)
    for k in range(1, HALO + 1):
        full[away == k] = np.float32(TAPS[k])
    high = full.astype(ml_dtypes.bfloat16)
    low = (full - high.astype(np.float32)).astype(ml_dtypes.bfloat16)
    halo = np.zeros((LX, LX), ml_dtypes.bfloat16)
    for start, part in ((0, high), (QUAD, high), (2 * QUAD, low)):
        halo[start : start + 2 * HALO] = part[LX:]
    return np.concatenate([high[:LX], halo, high[:LX], low[:LX]], axis=0)


def split(value):
    high = value.astype(BF16)
    return high, (value - high.astype(F32)).astype(BF16)


def filter_kernel(
    orb_hbm, pot_hbm, w_hbm, last, gram_ref,
    load, buf0, buf1, buf2, pack0, pack1, pack2, from_left, from_right, pv, w_ref, part, seen, word,
    load_sem, small_sem, ysend, yrecv, xsend, xrecv, zsend, zrecv, gsend, grecv,
):
    bufs, packs = (buf0, buf1, buf2), (pack0, pack1, pack2)
    sizes = {axis: lax.axis_size(axis) for axis in AXES}
    here = {axis: lax.axis_index(axis) for axis in AXES}

    def at(axis, step):
        return {axis: lax.rem(here[axis] + (step + sizes[axis]), sizes[axis])}

    neighbours = [(axis, step) for axis in ("gy", "gz", "gx") for step in (1, -1)]
    barrier = pltpu.get_barrier_semaphore()
    for axis, step in neighbours:
        pl.semaphore_signal(barrier, inc=1, device_id=at(axis, step), device_id_type=MESH)

    def load_copy(g, c):
        part = (pl.ds(g * SUB, SUB), pl.ds(c * SLABS * LY, SLABS * LY))
        return pltpu.make_async_copy(
            orb_hbm.at[part], load.at[part], load_sem.at[g * CHUNKS + c]
        )

    small = [
        pltpu.make_async_copy(pot_hbm, pv, small_sem.at[0]),
        pltpu.make_async_copy(w_hbm, w_ref, small_sem.at[1]),
    ]
    for g in range(GROUPS):
        for c in range(CHUNKS):
            load_copy(g, c).start()
    for copy in small:
        copy.start()

    def remote(src, dst, send_sem, recv_sem, axis, step):
        return pltpu.make_async_remote_copy(
            src_ref=src, dst_ref=dst, send_sem=send_sem, recv_sem=recv_sem,
            device_id=at(axis, step), device_id_type=MESH,
        )

    def y_copies(level, g, c):
        u, zs = g * CHUNKS + c, pl.ds(HALO + c * SLABS, SLABS)
        level_buf = bufs[level].at[g, zs]
        return [
            remote(
                level_buf.at[:, pl.ds(LY, HALO)], level_buf.at[:, pl.ds(0, HALO)],
                ysend.at[level, u, 0], yrecv.at[level, u, 0], "gy", 1,
            ),
            remote(
                level_buf.at[:, pl.ds(HALO, HALO)], level_buf.at[:, pl.ds(HALO + LY, HALO)],
                ysend.at[level, u, 1], yrecv.at[level, u, 1], "gy", -1,
            ),
        ]

    def x_copies(level, g, c):
        u, zs = g * CHUNKS + c, pl.ds(c * SLABS, SLABS)
        return [
            remote(
                packs[level].at[g, zs], from_left.at[level, g, zs],
                xsend.at[level, u, 0], xrecv.at[level, u, 0], "gx", 1,
            ),
            remote(
                packs[level].at[g, zs], from_right.at[level, g, zs],
                xsend.at[level, u, 1], xrecv.at[level, u, 1], "gx", -1,
            ),
        ]

    def z_copy(level, g, up):
        inner = pl.ds(HALO, LY)
        src, dst = (LZ, 0) if up else (HALO, HALO + LZ)
        i = 0 if up else 1
        return remote(
            bufs[level].at[g, pl.ds(src, HALO), inner],
            bufs[level].at[g, pl.ds(dst, HALO), inner],
            zsend.at[level, g, i], zrecv.at[level, g, i], "gz", 1 if up else -1,
        )

    def send(level, g, c):
        for copy in y_copies(level, g, c):
            copy.start()

        @pl.when(c == 0)
        def _():
            z_copy(level, g, False).start()

        @pl.when(c == CHUNKS - 1)
        def _():
            z_copy(level, g, True).start()

        for copy in x_copies(level, g, c):
            copy.start()

    lane = lax.broadcasted_iota(jnp.int32, (SUB, LX), 1)

    def pack_edges(values):
        packed = jnp.zeros((SUB, LX), F32)
        for y in range(LY):
            moved = pltpu.roll(values[y], 2 * HALO * y + HALO, 1)
            mine = (lane >= 2 * HALO * y) & (lane < 2 * HALO * (y + 1))
            packed = jnp.where(mine, moved, packed)
        return packed

    flat = load.reshape(NORB * ROWS, LX)

    def start_unit(g, c):
        load_copy(g, c).wait()

        @pl.loop(0, SLABS, unroll=UNROLL)
        def _(s):
            z = c * SLABS + s
            values = []
            for y in range(LY):
                v = flat[pl.ds(g * SUB * ROWS + z * LY + y, SUB, stride=ROWS), :]
                buf0[g, HALO + z, HALO + y] = v
                values.append(v)
            pack0[g, z] = pack_edges(values)

    start_unit(0, 0)
    pl.semaphore_wait(barrier, len(neighbours))
    send(0, 0, 0)

    @pl.loop(1, UNITS)
    def _(u):
        g, c = u // CHUNKS, lax.rem(u, CHUNKS)
        start_unit(g, c)
        send(0, g, c)

    for copy in small:
        copy.wait()
    pv[...] = pv[...] * F32(0.1) + F32(3.0 * TAPS[0] - 2.3)

    def stencil(level, g, z, y_halo=True):
        buf = bufs[level]
        edges = jnp.where(
            lax.rem(lane, 2 * HALO) < HALO, from_left[level, g, z], from_right[level, g, z]
        )
        edge_high = edges.astype(BF16).astype(F32)
        parts = (
            edge_high,
            pltpu.roll(edges - edge_high, QUAD, 1),
            pltpu.roll(edge_high, 2 * QUAD, 1),
        )
        halo = []
        for quad in range(LX // QUAD):
            own = parts[2]
            for i in (1, 0):
                own = jnp.where(lane // QUAD == (quad + i) % (LX // QUAD), parts[i], own)
            for y in range(QUAD // 8 * quad, QUAD // 8 * (quad + 1)):
                halo.append(pltpu.roll(own, (LX - 2 * HALO * y) % LX, 1))
        centre = [buf[g, HALO + z, HALO + y] for y in range(LY)]
        high, low = split(jnp.concatenate(centre, axis=0))
        rows = jnp.concatenate(
            [high, jnp.concatenate(halo, axis=0).astype(BF16), low, high], axis=1
        )
        along_x = jnp.dot(rows, w_ref[...], preferred_element_type=F32)
        out = []
        for y in range(LY):
            total = pv[z, pl.ds(y, 1), :] * centre[y] + along_x[y * SUB : (y + 1) * SUB]
            for k in range(1, HALO + 1):
                around = buf[g, HALO + z + k, HALO + y] + buf[g, HALO + z - k, HALO + y]
                rows_k = [r for r in (y + k, y - k) if y_halo or 0 <= r < LY]
                if rows_k:
                    beside = buf[g, HALO + z, HALO + rows_k[0]]
                    for r in rows_k[1:]:
                        beside = beside + buf[g, HALO + z, HALO + r]
                    around = around + beside
                total = total + F32(TAPS[k]) * around
            out.append(total)
        return out

    def wait_y(level, g, c):
        for copy in y_copies(level, g, c):
            copy.wait_recv()

    def wait_xz(level, g, c):
        for copy in x_copies(level, g, c):
            copy.wait_recv()

        @pl.when(c == 0)
        def _():
            z_copy(level, g, True).wait_recv()

        @pl.when(c == CHUNKS - 1)
        def _():
            z_copy(level, g, False).wait_recv()

    rounds = (
        [("gx", d) for d in range(1, sizes["gx"])],
        [("gy", d) for d in range(1, sizes["gy"])],
        [("gz", 2), ("gz", -2)],
        [("gz", d) for d in range(4, sizes["gz"] - 3, 2)],
    )

    def tell(i):
        for axis, step in rounds[i]:
            pl.semaphore_signal(
                word.at[i], inc=1, device_id=at(axis, step), device_id_type=MESH
            )

    def hear(i):
        pl.semaphore_wait(word.at[i], len(rounds[i]))

    for level in (1, 2):
        if level == 2:
            tell(0)

        @pl.loop(0, UNITS)
        def _(u, level=level):
            g, c = u // CHUNKS, lax.rem(u, CHUNKS)
            wait_y(level - 1, g, c)
            wait_xz(level - 1, g, c)

            if level == 2:

                @pl.when(u == CHUNKS)
                def _():
                    hear(0)
                    tell(1)

            @pl.loop(0, SLABS, unroll=UNROLL)
            def _(s):
                z = c * SLABS + s
                new = stencil(level - 1, g, z)
                if level == 1:
                    new = [F32(0.5) * v for v in new]
                else:
                    new = [v - buf0[g, HALO + z, HALO + y] for y, v in enumerate(new)]
                for y in range(LY):
                    bufs[level][g, HALO + z, HALO + y] = new[y]
                packs[level][g, z] = pack_edges(new)

            send(level, g, c)

    hear(1)
    tell(2)
    part[...] = jnp.zeros_like(part)

    def add_gram(g, zs, ys):
        @pl.when(g == GROUPS - 1)
        def _():
            total = jnp.zeros((2 * NORB, 2 * NORB), F32)
            for z in zs:
                wide = jnp.concatenate(
                    [
                        jnp.concatenate([last[k, z, y] for k in range(GROUPS)], axis=0)
                        for y in ys
                    ],
                    axis=1,
                )
                both = jnp.concatenate(split(wide), axis=0)
                total += lax.dot_general(
                    both, both, (((1,), (1,)), ((), ())), preferred_element_type=F32
                )
            four = total[:NORB] + total[NORB:]
            part[:, :NORB] += four[:, :NORB] + four[:, NORB:]

    @pl.loop(0, UNITS)
    def _(u):
        g, c = u // CHUNKS, lax.rem(u, CHUNKS)
        wait_xz(2, g, c)

        @pl.when(u == CHUNKS)
        def _():
            hear(2)
            tell(3)

        zs = [c * SLABS + s for s in range(SLABS)]
        for z in zs:
            new = stencil(2, g, z, y_halo=False)
            for y in range(LY):
                last[g, z, y] = new[y] - buf1[g, HALO + z, HALO + y]
        add_gram(g, zs, range(HALO, LY - HALO))

    @pl.loop(0, UNITS)
    def _(u):
        g, c = u // CHUNKS, lax.rem(u, CHUNKS)
        zs = [c * SLABS + s for s in range(SLABS)]
        wait_y(2, g, c)
        edge = [*range(HALO), *range(LY - HALO, LY)]
        for z in zs:
            for y in edge:
                total = last[g, z, y]
                for k in range(1, HALO + 1):
                    for r in (y + k, y - k):
                        if not 0 <= r < LY:
                            total = total + F32(TAPS[k]) * buf2[g, HALO + z, HALO + r]
                last[g, z, y] = total
        add_gram(g, zs, edge)

    def wait_sends():
        @pl.loop(0, UNITS)
        def _(u):
            g, c = u // CHUNKS, lax.rem(u, CHUNKS)
            for level in range(3):
                for copy in y_copies(level, g, c) + x_copies(level, g, c):
                    copy.wait_send()

        for level in range(3):
            for g in range(GROUPS):
                for up in (False, True):
                    z_copy(level, g, up).wait_send()

    hear(3)
    moved = pltpu.roll(part[...] * F32(1.0 / CELLS), 0, 1, stride=NORB, stride_axis=0)
    mine = (here["gx"] * sizes["gy"] + here["gy"]) * sizes["gz"] + here["gz"]
    seen[mine] = jnp.sum(moved.reshape(2, SUB, LX), axis=1)
    offsets = [
        (dx, dy, dz)
        for dx in range(sizes["gx"])
        for dy in range(sizes["gy"])
        for dz in range(sizes["gz"])
    ][1:]

    def hops(offset):
        dx, dy, dz = (min(d, sizes[axis] - d) for d, axis in zip(offset, AXES))
        return 2 * (dx + dy) + dz

    along = {axis: [at(axis, d)[axis] for d in range(sizes[axis])] for axis in AXES}
    for offset in sorted(offsets, key=hops, reverse=True):
        pltpu.make_async_remote_copy(
            src_ref=seen.at[mine], dst_ref=seen.at[mine], send_sem=gsend.at[0],
            recv_sem=grecv.at[0],
            device_id={axis: along[axis][d] for axis, d in zip(AXES, offset)},
            device_id_type=MESH,
        ).start()
    wait_sends()
    others = seen.at[pl.ds(0, len(offsets))]
    pltpu.make_async_copy(others, others, grecv.at[0]).wait()
    terms = [seen[k] for k in range(len(offsets) + 1)]
    while len(terms) > 1:
        terms = [a + b for a, b in zip(terms[::2], terms[1::2])]
    value = terms[0]
    gram_ref[...] = value
    pltpu.make_async_copy(others, others, gsend.at[0]).wait()


def solve_kernel(filt, gram_ref, out_hbm, factor_hbm, out, factor_ref, out_sem, factor_sem):
    def entry(i, j):
        at = NORB * (i % SUB) + j
        return jnp.broadcast_to(gram_ref[i // SUB : i // SUB + 1, at : at + 1], (SUB, LX))

    row = lax.broadcasted_iota(jnp.int32, (SUB, LX), 0)
    lane = lax.broadcasted_iota(jnp.int32, (SUB, LX), 1)
    lower, inverse = {}, []
    for j in range(NORB):
        column = {i: entry(i, j) for i in range(j, NORB)}
        for k in range(j):
            for i in range(j, NORB):
                column[i] = column[i] - lower[i, k] * lower[j, k]
        root = jnp.sqrt(column[j])
        scale = F32(1) / root
        lower[j, j] = root
        for i in range(j + 1, NORB):
            lower[i, j] = column[i] * scale
        line = jnp.where(lane == j, F32(1), F32(0))
        for m in range(j):
            line = line - lower[j, m] * inverse[m]
        inverse.append(line * scale)

    def stack(lines):
        halves = []
        for half in range(GROUPS):
            rows = lines[half * SUB]
            for i in range(1, SUB):
                rows = jnp.where(row == i, lines[half * SUB + i], rows)
            halves.append(rows)
        return jnp.concatenate(halves, axis=0)

    def gather(entries):
        lines = []
        for i in range(NORB):
            line = jnp.zeros((SUB, LX), F32)
            for j in range(NORB):
                if (i, j) in entries:
                    line = jnp.where(lane == j, entries[i, j], line)
            lines.append(line)
        return stack(lines)

    high, low = split(stack(inverse)[:, :NORB])
    lhs = jnp.concatenate([high, high, low], axis=1)

    factor_ref[...] = gather({(j, i): value for (i, j), value in lower.items()})[:, :NORB]
    factor_copy = pltpu.make_async_copy(factor_ref, factor_hbm, factor_sem)

    def out_copy(c):
        part = pl.ds(c * STEP * LY, STEP * LY)
        return pltpu.make_async_copy(out.at[:, part], out_hbm.at[:, part], out_sem.at[c])

    for c in range(LZ // STEP):
        for z in range(c * STEP, (c + 1) * STEP):
            wide = jnp.concatenate(
                [
                    jnp.concatenate([filt[g, z, y] for g in range(GROUPS)], axis=0)
                    for y in range(LY)
                ],
                axis=1,
            )
            high, low = split(wide)
            solved = jnp.dot(
                lhs, jnp.concatenate([high, low, high], axis=0), preferred_element_type=F32
            )
            for g in range(GROUPS):
                for start in range(0, LY, SUB):
                    block = jnp.stack(
                        [
                            solved[g * SUB : (g + 1) * SUB, y * LX : (y + 1) * LX]
                            for y in range(start, start + SUB)
                        ]
                    )
                    out[pl.ds(g * SUB, SUB), pl.ds(z * LY + start, SUB), :] = jnp.swapaxes(
                        block, 0, 1
                    )
        out_copy(c).start()
        if c == 0:
            factor_copy.start()
    factor_copy.wait()
    for c in range(LZ // STEP):
        out_copy(c).wait()


def on_device(orbitals, potential):
    hbm = pl.BlockSpec(memory_space=pltpu.HBM)
    vmem = pl.BlockSpec(memory_space=pltpu.VMEM)
    dma = pltpu.SemaphoreType.DMA
    sizes = {axis: lax.axis_size(axis) for axis in AXES}
    filtered, gram = pl.pallas_call(
        filter_kernel,
        name="filter_and_gram",
        out_shape=[
            jax.ShapeDtypeStruct((GROUPS, LZ, LY, SUB, LX), F32),
            jax.ShapeDtypeStruct((2, LX), F32),
        ],
        in_specs=[hbm] * 3,
        out_specs=[vmem, vmem],
        scratch_shapes=[
            pltpu.VMEM((NORB, ROWS, LX), F32),
            *[pltpu.VMEM((GROUPS, LZ + 2 * HALO, LY + 2 * HALO, SUB, LX), F32)] * 3,
            *[pltpu.VMEM((GROUPS, LZ, SUB, LX), F32)] * 3,
            *[pltpu.VMEM((3, GROUPS, LZ, SUB, LX), F32)] * 2,
            pltpu.VMEM((LZ, LY, LX), F32),
            pltpu.VMEM((4 * LX, LX), BF16),
            pltpu.VMEM((NORB, LX), F32),
            pltpu.VMEM((sizes["gx"] * sizes["gy"] * sizes["gz"], 2, LX), F32),
            pltpu.SemaphoreType.REGULAR((4,)),
            dma((UNITS,)),
            dma((2,)),
            dma((3, UNITS, 2)),
            dma((3, UNITS, 2)),
            dma((3, UNITS, 2)),
            dma((3, UNITS, 2)),
            dma((3, GROUPS, 2)),
            dma((3, GROUPS, 2)),
            dma((1,)),
            dma((1,)),
        ],
        compiler_params=pltpu.CompilerParams(
            collective_id=0, has_side_effects=True, vmem_limit_bytes=40 * 2**20
        ),
        cost_estimate=pl.CostEstimate(
            flops=10**9, bytes_accessed=5 * 2**20, transcendentals=0
        ),
    )(*[
        pltpu.with_memory_space_constraint(value, pltpu.HBM)
        for value in (
            orbitals.reshape(NORB, ROWS, LX), potential, jnp.asarray(x_weights())
        )
    ])
    solved, factor = pl.pallas_call(
        solve_kernel,
        name="solve",
        out_shape=[
            jax.ShapeDtypeStruct((NORB, ROWS, LX), F32),
            jax.ShapeDtypeStruct((NORB, NORB), F32),
        ],
        in_specs=[vmem, vmem],
        out_specs=[hbm, hbm],
        scratch_shapes=[
            pltpu.VMEM((NORB, ROWS, LX), F32),
            pltpu.VMEM((NORB, NORB), F32),
            dma((LZ // STEP,)),
            dma(()),
        ],
        compiler_params=pltpu.CompilerParams(vmem_limit_bytes=24 * 2**20),
        cost_estimate=pl.CostEstimate(
            flops=10**8, bytes_accessed=4 * 2**20, transcendentals=0
        ),
    )(filtered, gram)
    return solved.reshape(NORB, LZ, LY, LX), factor


def solution(mesh):
    in_specs = (P(None, "gz", "gy", "gx"), P("gz", "gy", "gx"))
    out_specs = (P(None, "gz", "gy", "gx"), P())
    return jax.shard_map(
        on_device, mesh=mesh, in_specs=in_specs, out_specs=out_specs, check_vma=False
    )
```

```python
import functools

import jax
import jax.numpy as jnp
import ml_dtypes
import numpy as np
from jax import lax
from jax.experimental import pallas as pl
from jax.experimental.pallas import tpu as pltpu
from jax.sharding import PartitionSpec as P

COEFFS = (-205.0 / 72.0, 8.0 / 5.0, -1.0 / 5.0, 8.0 / 315.0, -1.0 / 560.0)
SCALE = 2.0 * -2.0 / 20.0
TAPS = tuple(SCALE * c for c in COEFFS)

NORB, LZ, LY, LX = 16, 16, 16, 128
HALO = 4
SUB = 8
GROUPS = NORB // SUB
SLABS = 4
CHUNKS = LZ // SLABS
UNITS = GROUPS * CHUNKS
QUAD = 8 * HALO
UNROLL = 4
STEP = 2
ROWS = LZ * LY
PITCH = ROWS + SUB
CELLS = 4194304
F32, BF16 = jnp.float32, jnp.bfloat16
MESH = pl.DeviceIdType.MESH
AXES = ("gx", "gy", "gz")


def x_weights():
    places = np.concatenate([np.arange(LX), np.arange(-HALO, 0), np.arange(LX, LX + HALO)])
    away = np.abs(places[:, None] - np.arange(LX)[None, :])
    full = np.zeros((LX + 2 * HALO, LX), np.float32)
    for k in range(1, HALO + 1):
        full[away == k] = np.float32(TAPS[k])
    high = full.astype(ml_dtypes.bfloat16)
    low = (full - high.astype(np.float32)).astype(ml_dtypes.bfloat16)
    halo = np.zeros((LX, LX), ml_dtypes.bfloat16)
    for start, part in ((0, high), (QUAD, high), (2 * QUAD, low)):
        halo[start : start + 2 * HALO] = part[LX:]
    return np.concatenate([high[:LX], halo, high[:LX], low[:LX]], axis=0)


def split(value):
    high = value.astype(BF16)
    return high, (value - high.astype(F32)).astype(BF16)


def filter_kernel(
    orb_hbm, pot_hbm, w_hbm, last, gram_ref,
    load, buf0, buf1, buf2, pack0, pack1, pack2, from_left, from_right, pv, w_ref, part, seen, word,
    load_sem, small_sem, ysend, yrecv, xsend, xrecv, zsend, zrecv, gsend, grecv,
):
    bufs, packs = (buf0, buf1, buf2), (pack0, pack1, pack2)
    sizes = {axis: lax.axis_size(axis) for axis in AXES}
    here = {axis: lax.axis_index(axis) for axis in AXES}

    def at(axis, step):
        return {axis: lax.rem(here[axis] + (step + sizes[axis]), sizes[axis])}

    neighbours = [(axis, step) for axis in ("gy", "gz", "gx") for step in (1, -1)]
    barrier = pltpu.get_barrier_semaphore()
    for axis, step in neighbours:
        pl.semaphore_signal(barrier, inc=1, device_id=at(axis, step), device_id_type=MESH)

    def load_copy(g, c):
        part = (pl.ds(g * SUB, SUB), pl.ds(c * SLABS * LY, SLABS * LY))
        return pltpu.make_async_copy(
            orb_hbm.at[part], load.at[part], load_sem.at[g * CHUNKS + c]
        )

    small = [
        pltpu.make_async_copy(pot_hbm, pv, small_sem.at[0]),
        pltpu.make_async_copy(w_hbm, w_ref, small_sem.at[1]),
    ]
    for g in range(GROUPS):
        for c in range(CHUNKS):
            load_copy(g, c).start()
    for copy in small:
        copy.start()

    def remote(src, dst, send_sem, recv_sem, axis, step):
        return pltpu.make_async_remote_copy(
            src_ref=src, dst_ref=dst, send_sem=send_sem, recv_sem=recv_sem,
            device_id=at(axis, step), device_id_type=MESH,
        )

    def y_copies(level, g, c):
        u, zs = g * CHUNKS + c, pl.ds(HALO + c * SLABS, SLABS)
        level_buf = bufs[level].at[g, zs]
        return [
            remote(
                level_buf.at[:, pl.ds(LY, HALO)], level_buf.at[:, pl.ds(0, HALO)],
                ysend.at[level, u, 0], yrecv.at[level, u, 0], "gy", 1,
            ),
            remote(
                level_buf.at[:, pl.ds(HALO, HALO)], level_buf.at[:, pl.ds(HALO + LY, HALO)],
                ysend.at[level, u, 1], yrecv.at[level, u, 1], "gy", -1,
            ),
        ]

    def x_copies(level, g, c):
        u, zs = g * CHUNKS + c, pl.ds(c * SLABS, SLABS)
        return [
            remote(
                packs[level].at[g, zs], from_left.at[level, g, zs],
                xsend.at[level, u, 0], xrecv.at[level, u, 0], "gx", 1,
            ),
            remote(
                packs[level].at[g, zs], from_right.at[level, g, zs],
                xsend.at[level, u, 1], xrecv.at[level, u, 1], "gx", -1,
            ),
        ]

    def z_copy(level, g, up):
        inner = pl.ds(HALO, LY)
        src, dst = (LZ, 0) if up else (HALO, HALO + LZ)
        i = 0 if up else 1
        return remote(
            bufs[level].at[g, pl.ds(src, HALO), inner],
            bufs[level].at[g, pl.ds(dst, HALO), inner],
            zsend.at[level, g, i], zrecv.at[level, g, i], "gz", 1 if up else -1,
        )

    def send(level, g, c):
        for copy in y_copies(level, g, c):
            copy.start()

        @pl.when(c == 0)
        def _():
            z_copy(level, g, False).start()

        @pl.when(c == CHUNKS - 1)
        def _():
            z_copy(level, g, True).start()

        for copy in x_copies(level, g, c):
            copy.start()

    lane = lax.broadcasted_iota(jnp.int32, (SUB, LX), 1)

    def pack_edges(values):
        packed = jnp.zeros((SUB, LX), F32)
        for y in range(LY):
            moved = pltpu.roll(values[y], 2 * HALO * y + HALO, 1)
            mine = (lane >= 2 * HALO * y) & (lane < 2 * HALO * (y + 1))
            packed = jnp.where(mine, moved, packed)
        return packed

    flat = load.reshape((NORB + 1) * PITCH, LX)

    def start_unit(g, c):
        load_copy(g, c).wait()

        @pl.loop(0, SLABS, unroll=UNROLL)
        def _(s):
            z = c * SLABS + s
            values = []
            for y in range(LY):
                v = flat[pl.ds(g * SUB * PITCH + z * LY + y, SUB, stride=PITCH), :]
                buf0[g, HALO + z, HALO + y] = v
                values.append(v)
            pack0[g, z] = pack_edges(values)

    start_unit(0, 0)
    pl.semaphore_wait(barrier, len(neighbours))
    send(0, 0, 0)

    @pl.loop(1, UNITS)
    def _(u):
        g, c = u // CHUNKS, lax.rem(u, CHUNKS)
        start_unit(g, c)
        send(0, g, c)

    for copy in small:
        copy.wait()
    pv[...] = pv[...] * F32(0.1) + F32(3.0 * TAPS[0] - 2.3)

    def stencil(level, g, z, y_halo=True):
        buf = bufs[level]
        edges = jnp.where(
            lax.rem(lane, 2 * HALO) < HALO, from_left[level, g, z], from_right[level, g, z]
        )
        edge_high = edges.astype(BF16).astype(F32)
        parts = (
            edge_high,
            pltpu.roll(edges - edge_high, QUAD, 1),
            pltpu.roll(edge_high, 2 * QUAD, 1),
        )
        halo = []
        for quad in range(LX // QUAD):
            own = parts[2]
            for i in (1, 0):
                own = jnp.where(lane // QUAD == (quad + i) % (LX // QUAD), parts[i], own)
            for y in range(QUAD // 8 * quad, QUAD // 8 * (quad + 1)):
                halo.append(pltpu.roll(own, (LX - 2 * HALO * y) % LX, 1))
        centre = [buf[g, HALO + z, HALO + y] for y in range(LY)]
        high, low = split(jnp.concatenate(centre, axis=0))
        rows = jnp.concatenate(
            [high, jnp.concatenate(halo, axis=0).astype(BF16), low, high], axis=1
        )
        along_x = jnp.dot(rows, w_ref[...], preferred_element_type=F32)
        out = []
        for y in range(LY):
            total = pv[z, pl.ds(y, 1), :] * centre[y] + along_x[y * SUB : (y + 1) * SUB]
            for k in range(1, HALO + 1):
                around = buf[g, HALO + z + k, HALO + y] + buf[g, HALO + z - k, HALO + y]
                rows_k = [r for r in (y + k, y - k) if y_halo or 0 <= r < LY]
                if rows_k:
                    beside = buf[g, HALO + z, HALO + rows_k[0]]
                    for r in rows_k[1:]:
                        beside = beside + buf[g, HALO + z, HALO + r]
                    around = around + beside
                total = total + F32(TAPS[k]) * around
            out.append(total)
        return out

    def wait_y(level, g, c):
        for copy in y_copies(level, g, c):
            copy.wait_recv()

    def wait_xz(level, g, c):
        for copy in x_copies(level, g, c):
            copy.wait_recv()

        @pl.when(c == 0)
        def _():
            z_copy(level, g, True).wait_recv()

        @pl.when(c == CHUNKS - 1)
        def _():
            z_copy(level, g, False).wait_recv()

    rounds = (
        [("gx", d) for d in range(1, sizes["gx"])],
        [("gy", d) for d in range(1, sizes["gy"])],
        [("gz", 2), ("gz", -2)],
        [("gz", d) for d in range(4, sizes["gz"] - 3, 2)],
    )

    def tell(i):
        for axis, step in rounds[i]:
            pl.semaphore_signal(
                word.at[i], inc=1, device_id=at(axis, step), device_id_type=MESH
            )

    def hear(i):
        pl.semaphore_wait(word.at[i], len(rounds[i]))

    for level in (1, 2):
        if level == 2:
            tell(0)

        @pl.loop(0, UNITS)
        def _(u, level=level):
            g, c = u // CHUNKS, lax.rem(u, CHUNKS)
            wait_y(level - 1, g, c)
            wait_xz(level - 1, g, c)

            if level == 2:

                @pl.when(u == CHUNKS)
                def _():
                    hear(0)
                    tell(1)

            @pl.loop(0, SLABS, unroll=UNROLL)
            def _(s):
                z = c * SLABS + s
                new = stencil(level - 1, g, z)
                if level == 1:
                    new = [F32(0.5) * v for v in new]
                else:
                    new = [v - buf0[g, HALO + z, HALO + y] for y, v in enumerate(new)]
                for y in range(LY):
                    bufs[level][g, HALO + z, HALO + y] = new[y]
                packs[level][g, z] = pack_edges(new)

            send(level, g, c)

    hear(1)
    tell(2)
    part[...] = jnp.zeros_like(part)

    def add_gram(g, zs, ys):
        @pl.when(g == GROUPS - 1)
        def _():
            total = jnp.zeros((2 * NORB, 2 * NORB), F32)
            for z in zs:
                wide = jnp.concatenate(
                    [
                        jnp.concatenate([last[k, z, y] for k in range(GROUPS)], axis=0)
                        for y in ys
                    ],
                    axis=1,
                )
                both = jnp.concatenate(split(wide), axis=0)
                total += lax.dot_general(
                    both, both, (((1,), (1,)), ((), ())), preferred_element_type=F32
                )
            four = total[:NORB] + total[NORB:]
            part[:, :NORB] += four[:, :NORB] + four[:, NORB:]

    @pl.loop(0, UNITS)
    def _(u):
        g, c = u // CHUNKS, lax.rem(u, CHUNKS)
        wait_xz(2, g, c)

        @pl.when(u == CHUNKS)
        def _():
            hear(2)
            tell(3)

        zs = [c * SLABS + s for s in range(SLABS)]
        for z in zs:
            new = stencil(2, g, z, y_halo=False)
            for y in range(LY):
                last[g, z, y] = new[y] - buf1[g, HALO + z, HALO + y]
        add_gram(g, zs, range(HALO, LY - HALO))

    @pl.loop(0, UNITS)
    def _(u):
        g, c = u // CHUNKS, lax.rem(u, CHUNKS)
        zs = [c * SLABS + s for s in range(SLABS)]
        wait_y(2, g, c)
        edge = [*range(HALO), *range(LY - HALO, LY)]
        for z in zs:
            for y in edge:
                total = last[g, z, y]
                for k in range(1, HALO + 1):
                    for r in (y + k, y - k):
                        if not 0 <= r < LY:
                            total = total + F32(TAPS[k]) * buf2[g, HALO + z, HALO + r]
                last[g, z, y] = total
        add_gram(g, zs, edge)

    def wait_sends():
        @pl.loop(0, UNITS)
        def _(u):
            g, c = u // CHUNKS, lax.rem(u, CHUNKS)
            for level in range(3):
                for copy in y_copies(level, g, c) + x_copies(level, g, c):
                    copy.wait_send()

        for level in range(3):
            for g in range(GROUPS):
                for up in (False, True):
                    z_copy(level, g, up).wait_send()

    hear(3)
    moved = pltpu.roll(part[...] * F32(1.0 / CELLS), 0, 1, stride=NORB, stride_axis=0)
    mine = (here["gx"] * sizes["gy"] + here["gy"]) * sizes["gz"] + here["gz"]
    seen[mine] = jnp.sum(moved.reshape(2, SUB, LX), axis=1)
    offsets = [
        (dx, dy, dz)
        for dx in range(sizes["gx"])
        for dy in range(sizes["gy"])
        for dz in range(sizes["gz"])
    ][1:]

    def hops(offset):
        dx, dy, dz = (min(d, sizes[axis] - d) for d, axis in zip(offset, AXES))
        return 2 * (dx + dy) + dz

    along = {axis: [at(axis, d)[axis] for d in range(sizes[axis])] for axis in AXES}
    for offset in sorted(offsets, key=hops, reverse=True):
        pltpu.make_async_remote_copy(
            src_ref=seen.at[mine], dst_ref=seen.at[mine], send_sem=gsend.at[0],
            recv_sem=grecv.at[0],
            device_id={axis: along[axis][d] for axis, d in zip(AXES, offset)},
            device_id_type=MESH,
        ).start()
    wait_sends()
    others = seen.at[pl.ds(0, len(offsets))]
    pltpu.make_async_copy(others, others, grecv.at[0]).wait()
    terms = [seen[k] for k in range(len(offsets) + 1)]
    while len(terms) > 1:
        terms = [a + b for a, b in zip(terms[::2], terms[1::2])]
    value = terms[0]
    gram_ref[...] = value
    pltpu.make_async_copy(others, others, gsend.at[0]).wait()


def solve_kernel(filt, gram_ref, out_hbm, factor_hbm, out, factor_ref, out_sem, factor_sem):
    def entry(i, j):
        at = NORB * (i % SUB) + j
        return jnp.broadcast_to(gram_ref[i // SUB : i // SUB + 1, at : at + 1], (SUB, LX))

    row = lax.broadcasted_iota(jnp.int32, (SUB, LX), 0)
    lane = lax.broadcasted_iota(jnp.int32, (SUB, LX), 1)
    lower, inverse = {}, []
    for j in range(NORB):
        column = {i: entry(i, j) for i in range(j, NORB)}
        for k in range(j):
            for i in range(j, NORB):
                column[i] = column[i] - lower[i, k] * lower[j, k]
        root = jnp.sqrt(column[j])
        scale = F32(1) / root
        lower[j, j] = root
        for i in range(j + 1, NORB):
            lower[i, j] = column[i] * scale
        line = jnp.where(lane == j, F32(1), F32(0))
        for m in range(j):
            line = line - lower[j, m] * inverse[m]
        inverse.append(line * scale)

    def stack(lines):
        halves = []
        for half in range(GROUPS):
            rows = lines[half * SUB]
            for i in range(1, SUB):
                rows = jnp.where(row == i, lines[half * SUB + i], rows)
            halves.append(rows)
        return jnp.concatenate(halves, axis=0)

    def gather(entries):
        lines = []
        for i in range(NORB):
            line = jnp.zeros((SUB, LX), F32)
            for j in range(NORB):
                if (i, j) in entries:
                    line = jnp.where(lane == j, entries[i, j], line)
            lines.append(line)
        return stack(lines)

    high, low = split(stack(inverse)[:, :NORB])
    lhs = jnp.concatenate([high, high, low], axis=1)

    factor_ref[...] = gather({(j, i): value for (i, j), value in lower.items()})[:, :NORB]
    factor_copy = pltpu.make_async_copy(factor_ref, factor_hbm, factor_sem)

    def out_copy(c):
        part = pl.ds(c * STEP * LY, STEP * LY)
        return pltpu.make_async_copy(out.at[:, part], out_hbm.at[:, part], out_sem.at[c])

    for c in range(LZ // STEP):
        for z in range(c * STEP, (c + 1) * STEP):
            wide = jnp.concatenate(
                [
                    jnp.concatenate([filt[g, z, y] for g in range(GROUPS)], axis=0)
                    for y in range(LY)
                ],
                axis=1,
            )
            high, low = split(wide)
            solved = jnp.dot(
                lhs, jnp.concatenate([high, low, high], axis=0), preferred_element_type=F32
            )
            for g in range(GROUPS):
                for start in range(0, LY, SUB):
                    block = jnp.stack(
                        [
                            solved[g * SUB : (g + 1) * SUB, y * LX : (y + 1) * LX]
                            for y in range(start, start + SUB)
                        ]
                    )
                    out[pl.ds(g * SUB, SUB), pl.ds(z * LY + start, SUB), :] = jnp.swapaxes(
                        block, 0, 1
                    )
        out_copy(c).start()
        if c == 0:
            factor_copy.start()
    factor_copy.wait()
    for c in range(LZ // STEP):
        out_copy(c).wait()


def on_device(orbitals, potential):
    hbm = pl.BlockSpec(memory_space=pltpu.HBM)
    vmem = pl.BlockSpec(memory_space=pltpu.VMEM)
    dma = pltpu.SemaphoreType.DMA
    sizes = {axis: lax.axis_size(axis) for axis in AXES}
    filtered, gram = pl.pallas_call(
        filter_kernel,
        name="filter_and_gram",
        out_shape=[
            jax.ShapeDtypeStruct((GROUPS, LZ, LY, SUB, LX), F32),
            jax.ShapeDtypeStruct((2, LX), F32),
        ],
        in_specs=[hbm] * 3,
        out_specs=[vmem, vmem],
        scratch_shapes=[
            pltpu.VMEM((NORB + 1, PITCH, LX), F32),
            *[pltpu.VMEM((GROUPS, LZ + 2 * HALO, LY + 2 * HALO, SUB, LX), F32)] * 3,
            *[pltpu.VMEM((GROUPS, LZ, SUB, LX), F32)] * 3,
            *[pltpu.VMEM((3, GROUPS, LZ, SUB, LX), F32)] * 2,
            pltpu.VMEM((LZ, LY, LX), F32),
            pltpu.VMEM((4 * LX, LX), BF16),
            pltpu.VMEM((NORB, LX), F32),
            pltpu.VMEM((sizes["gx"] * sizes["gy"] * sizes["gz"], 2, LX), F32),
            pltpu.SemaphoreType.REGULAR((4,)),
            dma((UNITS,)),
            dma((2,)),
            dma((3, UNITS, 2)),
            dma((3, UNITS, 2)),
            dma((3, UNITS, 2)),
            dma((3, UNITS, 2)),
            dma((3, GROUPS, 2)),
            dma((3, GROUPS, 2)),
            dma((1,)),
            dma((1,)),
        ],
        compiler_params=pltpu.CompilerParams(
            collective_id=0, has_side_effects=True, vmem_limit_bytes=40 * 2**20
        ),
        cost_estimate=pl.CostEstimate(
            flops=10**9, bytes_accessed=5 * 2**20, transcendentals=0
        ),
    )(*[
        pltpu.with_memory_space_constraint(value, pltpu.HBM)
        for value in (
            orbitals.reshape(NORB, ROWS, LX), potential, jnp.asarray(x_weights())
        )
    ])
    solved, factor = pl.pallas_call(
        solve_kernel,
        name="solve",
        out_shape=[
            jax.ShapeDtypeStruct((NORB, ROWS, LX), F32),
            jax.ShapeDtypeStruct((NORB, NORB), F32),
        ],
        in_specs=[vmem, vmem],
        out_specs=[hbm, hbm],
        scratch_shapes=[
            pltpu.VMEM((NORB, ROWS, LX), F32),
            pltpu.VMEM((NORB, NORB), F32),
            dma((LZ // STEP,)),
            dma(()),
        ],
        compiler_params=pltpu.CompilerParams(vmem_limit_bytes=24 * 2**20),
        cost_estimate=pl.CostEstimate(
            flops=10**8, bytes_accessed=4 * 2**20, transcendentals=0
        ),
    )(filtered, gram)
    return solved.reshape(NORB, LZ, LY, LX), factor


def solution(mesh):
    in_specs = (P(None, "gz", "gy", "gx"), P("gz", "gy", "gx"))
    out_specs = (P(None, "gz", "gy", "gx"), P())
    return jax.shard_map(
        on_device, mesh=mesh, in_specs=in_specs, out_specs=out_specs, check_vma=False
    )
```

```python
import functools

import jax
import jax.numpy as jnp
import ml_dtypes
import numpy as np
from jax import lax
from jax.experimental import pallas as pl
from jax.experimental.pallas import tpu as pltpu
from jax.sharding import PartitionSpec as P

COEFFS = (-205.0 / 72.0, 8.0 / 5.0, -1.0 / 5.0, 8.0 / 315.0, -1.0 / 560.0)
SCALE = 2.0 * -2.0 / 20.0
TAPS = tuple(SCALE * c for c in COEFFS)

NORB, LZ, LY, LX = 16, 16, 16, 128
HALO = 4
SUB = 8
GROUPS = NORB // SUB
SLABS = 4
CHUNKS = LZ // SLABS
UNITS = GROUPS * CHUNKS
QUAD = 8 * HALO
UNROLL = 4
STEP = 2
ROWS = LZ * LY
CELLS = 4194304
F32, BF16 = jnp.float32, jnp.bfloat16
MESH = pl.DeviceIdType.MESH
AXES = ("gx", "gy", "gz")


def x_weights():
    places = np.concatenate([np.arange(LX), np.arange(-HALO, 0), np.arange(LX, LX + HALO)])
    away = np.abs(places[:, None] - np.arange(LX)[None, :])
    full = np.zeros((LX + 2 * HALO, LX), np.float32)
    for k in range(1, HALO + 1):
        full[away == k] = np.float32(TAPS[k])
    high = full.astype(ml_dtypes.bfloat16)
    low = (full - high.astype(np.float32)).astype(ml_dtypes.bfloat16)
    halo = np.zeros((LX, LX), ml_dtypes.bfloat16)
    for start, part in ((0, high), (QUAD, high), (2 * QUAD, low)):
        halo[start : start + 2 * HALO] = part[LX:]
    return np.concatenate([high[:LX], halo, high[:LX], low[:LX]], axis=0)


def split(value):
    high = value.astype(BF16)
    return high, (value - high.astype(F32)).astype(BF16)


def filter_kernel(
    orb_hbm, pot_hbm, w_hbm, last, gram_ref,
    load, buf0, buf1, buf2, pack0, pack1, pack2, from_left, from_right, pv, w_ref, part, seen, word,
    load_sem, small_sem, ysend, yrecv, xsend, xrecv, zsend, zrecv, gsend, grecv,
):
    bufs, packs = (buf0, buf1, buf2), (pack0, pack1, pack2)
    sizes = {axis: lax.axis_size(axis) for axis in AXES}
    here = {axis: lax.axis_index(axis) for axis in AXES}

    def at(axis, step):
        return {axis: lax.rem(here[axis] + (step + sizes[axis]), sizes[axis])}

    neighbours = [(axis, step) for axis in ("gy", "gz", "gx") for step in (1, -1)]
    barrier = pltpu.get_barrier_semaphore()
    for axis, step in neighbours:
        pl.semaphore_signal(barrier, inc=1, device_id=at(axis, step), device_id_type=MESH)

    def load_copy(g, c):
        part = (pl.ds(g * SUB, SUB), pl.ds(c * SLABS * LY, SLABS * LY))
        return pltpu.make_async_copy(
            orb_hbm.at[part], load.at[part], load_sem.at[g * CHUNKS + c]
        )

    small = [
        pltpu.make_async_copy(pot_hbm, pv, small_sem.at[0]),
        pltpu.make_async_copy(w_hbm, w_ref, small_sem.at[1]),
    ]
    for g in range(GROUPS):
        for c in range(CHUNKS):
            load_copy(g, c).start()
    for copy in small:
        copy.start()

    def remote(src, dst, send_sem, recv_sem, axis, step):
        return pltpu.make_async_remote_copy(
            src_ref=src, dst_ref=dst, send_sem=send_sem, recv_sem=recv_sem,
            device_id=at(axis, step), device_id_type=MESH,
        )

    def y_copies(level, g, c):
        u, zs = g * CHUNKS + c, pl.ds(HALO + c * SLABS, SLABS)
        level_buf = bufs[level].at[g, zs]
        return [
            remote(
                level_buf.at[:, pl.ds(LY, HALO)], level_buf.at[:, pl.ds(0, HALO)],
                ysend.at[level, u, 0], yrecv.at[level, u, 0], "gy", 1,
            ),
            remote(
                level_buf.at[:, pl.ds(HALO, HALO)], level_buf.at[:, pl.ds(HALO + LY, HALO)],
                ysend.at[level, u, 1], yrecv.at[level, u, 1], "gy", -1,
            ),
        ]

    def x_copies(level, g, c):
        u, zs = g * CHUNKS + c, pl.ds(c * SLABS, SLABS)
        return [
            remote(
                packs[level].at[g, zs], from_left.at[level, g, zs],
                xsend.at[level, u, 0], xrecv.at[level, u, 0], "gx", 1,
            ),
            remote(
                packs[level].at[g, zs], from_right.at[level, g, zs],
                xsend.at[level, u, 1], xrecv.at[level, u, 1], "gx", -1,
            ),
        ]

    def z_copy(level, g, up):
        inner = pl.ds(HALO, LY)
        src, dst = (LZ, 0) if up else (HALO, HALO + LZ)
        i = 0 if up else 1
        return remote(
            bufs[level].at[g, pl.ds(src, HALO), inner],
            bufs[level].at[g, pl.ds(dst, HALO), inner],
            zsend.at[level, g, i], zrecv.at[level, g, i], "gz", 1 if up else -1,
        )

    def send(level, g, c):
        for copy in y_copies(level, g, c):
            copy.start()

        @pl.when(c == 0)
        def _():
            z_copy(level, g, False).start()

        @pl.when(c == CHUNKS - 1)
        def _():
            z_copy(level, g, True).start()

        for copy in x_copies(level, g, c):
            copy.start()

    lane = lax.broadcasted_iota(jnp.int32, (SUB, LX), 1)

    def pack_edges(values):
        packed = jnp.zeros((SUB, LX), F32)
        for y in range(LY):
            moved = pltpu.roll(values[y], 2 * HALO * y + HALO, 1)
            mine = (lane >= 2 * HALO * y) & (lane < 2 * HALO * (y + 1))
            packed = jnp.where(mine, moved, packed)
        return packed

    flat = load.reshape(NORB * ROWS, LX)

    def start_unit(g, c):
        load_copy(g, c).wait()

        @pl.loop(0, SLABS, unroll=UNROLL)
        def _(s):
            z = c * SLABS + s
            values = []
            for y in range(LY):
                v = flat[pl.ds(g * SUB * ROWS + z * LY + y, SUB, stride=ROWS), :]
                buf0[g, HALO + z, HALO + y] = v
                values.append(v)
            pack0[g, z] = pack_edges(values)

    start_unit(0, 0)
    pl.semaphore_wait(barrier, len(neighbours))
    send(0, 0, 0)

    @pl.loop(1, UNITS)
    def _(u):
        g, c = u // CHUNKS, lax.rem(u, CHUNKS)
        start_unit(g, c)
        send(0, g, c)

    for copy in small:
        copy.wait()
    pv[...] = pv[...] * F32(0.1) + F32(3.0 * TAPS[0] - 2.3)

    def stencil(level, g, z, y_halo=True):
        buf = bufs[level]
        edges = jnp.where(
            lax.rem(lane, 2 * HALO) < HALO, from_left[level, g, z], from_right[level, g, z]
        )
        edge_high = edges.astype(BF16).astype(F32)
        parts = (
            edge_high,
            pltpu.roll(edges - edge_high, QUAD, 1),
            pltpu.roll(edge_high, 2 * QUAD, 1),
        )
        halo = []
        for quad in range(LX // QUAD):
            own = parts[2]
            for i in (1, 0):
                own = jnp.where(lane // QUAD == (quad + i) % (LX // QUAD), parts[i], own)
            for y in range(QUAD // 8 * quad, QUAD // 8 * (quad + 1)):
                halo.append(pltpu.roll(own, (LX - 2 * HALO * y) % LX, 1))
        centre = [buf[g, HALO + z, HALO + y] for y in range(LY)]
        high, low = split(jnp.concatenate(centre, axis=0))
        rows = jnp.concatenate(
            [high, jnp.concatenate(halo, axis=0).astype(BF16), low, high], axis=1
        )
        along_x = jnp.dot(rows, w_ref[...], preferred_element_type=F32)
        out = []
        for y in range(LY):
            total = pv[z, pl.ds(y, 1), :] * centre[y] + along_x[y * SUB : (y + 1) * SUB]
            for k in range(1, HALO + 1):
                around = buf[g, HALO + z + k, HALO + y] + buf[g, HALO + z - k, HALO + y]
                rows_k = [r for r in (y + k, y - k) if y_halo or 0 <= r < LY]
                if rows_k:
                    beside = buf[g, HALO + z, HALO + rows_k[0]]
                    for r in rows_k[1:]:
                        beside = beside + buf[g, HALO + z, HALO + r]
                    around = around + beside
                total = total + F32(TAPS[k]) * around
            out.append(total)
        return out

    def wait_y(level, g, c):
        for copy in y_copies(level, g, c):
            copy.wait_recv()

    def wait_xz(level, g, c):
        for copy in x_copies(level, g, c):
            copy.wait_recv()

        @pl.when(c == 0)
        def _():
            z_copy(level, g, True).wait_recv()

        @pl.when(c == CHUNKS - 1)
        def _():
            z_copy(level, g, False).wait_recv()

    rounds = (
        [("gx", d) for d in range(1, sizes["gx"])],
        [("gy", d) for d in range(1, sizes["gy"])],
        [("gz", 2), ("gz", -2)],
        [("gz", d) for d in range(4, sizes["gz"] - 3, 2)],
    )

    def tell(i):
        for axis, step in rounds[i]:
            pl.semaphore_signal(
                word.at[i], inc=1, device_id=at(axis, step), device_id_type=MESH
            )

    def hear(i):
        pl.semaphore_wait(word.at[i], len(rounds[i]))

    for level in (1, 2):
        if level == 2:
            tell(0)

        @pl.loop(0, UNITS)
        def _(u, level=level):
            g, c = u // CHUNKS, lax.rem(u, CHUNKS)
            wait_y(level - 1, g, c)
            wait_xz(level - 1, g, c)

            if level == 2:

                @pl.when(u == CHUNKS)
                def _():
                    hear(0)
                    tell(1)

            @pl.loop(0, SLABS, unroll=UNROLL)
            def _(s):
                z = c * SLABS + s
                new = stencil(level - 1, g, z)
                if level == 1:
                    new = [F32(0.5) * v for v in new]
                else:
                    new = [v - buf0[g, HALO + z, HALO + y] for y, v in enumerate(new)]
                for y in range(LY):
                    bufs[level][g, HALO + z, HALO + y] = new[y]
                packs[level][g, z] = pack_edges(new)

            send(level, g, c)

    hear(1)
    tell(2)
    part[...] = jnp.zeros_like(part)

    def add_gram(g, zs, ys):
        @pl.when(g == GROUPS - 1)
        def _():
            total = jnp.zeros((2 * NORB, 2 * NORB), F32)
            for z in zs:
                wide = jnp.concatenate(
                    [
                        jnp.concatenate([last[k, z, y] for k in range(GROUPS)], axis=0)
                        for y in ys
                    ],
                    axis=1,
                )
                both = jnp.concatenate(split(wide), axis=0)
                total += lax.dot_general(
                    both, both, (((1,), (1,)), ((), ())), preferred_element_type=F32
                )
            four = total[:NORB] + total[NORB:]
            part[:, :NORB] += four[:, :NORB] + four[:, NORB:]

    @pl.loop(0, UNITS)
    def _(u):
        g, c = u // CHUNKS, lax.rem(u, CHUNKS)
        wait_xz(2, g, c)

        @pl.when(u == CHUNKS)
        def _():
            hear(2)
            tell(3)

        zs = [c * SLABS + s for s in range(SLABS)]
        for z in zs:
            new = stencil(2, g, z, y_halo=False)
            for y in range(LY):
                last[g, z, y] = new[y] - buf1[g, HALO + z, HALO + y]
        add_gram(g, zs, range(HALO, LY - HALO))

    @pl.loop(0, UNITS)
    def _(u):
        g, c = u // CHUNKS, lax.rem(u, CHUNKS)
        zs = [c * SLABS + s for s in range(SLABS)]
        wait_y(2, g, c)
        edge = [*range(HALO), *range(LY - HALO, LY)]
        for z in zs:
            for y in edge:
                total = last[g, z, y]
                for k in range(1, HALO + 1):
                    for r in (y + k, y - k):
                        if not 0 <= r < LY:
                            total = total + F32(TAPS[k]) * buf2[g, HALO + z, HALO + r]
                last[g, z, y] = total
        add_gram(g, zs, edge)

    def wait_sends():
        @pl.loop(0, UNITS)
        def _(u):
            g, c = u // CHUNKS, lax.rem(u, CHUNKS)
            for level in range(3):
                for copy in y_copies(level, g, c) + x_copies(level, g, c):
                    copy.wait_send()

        for level in range(3):
            for g in range(GROUPS):
                for up in (False, True):
                    z_copy(level, g, up).wait_send()

    hear(3)
    moved = pltpu.roll(part[...] * F32(1.0 / CELLS), 0, 1, stride=NORB, stride_axis=0)
    mine = (here["gx"] * sizes["gy"] + here["gy"]) * sizes["gz"] + here["gz"]
    seen[mine] = jnp.sum(moved.reshape(2, SUB, LX), axis=1)
    offsets = [
        (dx, dy, dz)
        for dx in range(sizes["gx"])
        for dy in range(sizes["gy"])
        for dz in range(sizes["gz"])
    ][1:]

    def hops(offset):
        dx, dy, dz = (min(d, sizes[axis] - d) for d, axis in zip(offset, AXES))
        return 2 * (dx + dy) + dz

    along = {axis: [at(axis, d)[axis] for d in range(sizes[axis])] for axis in AXES}
    for offset in sorted(offsets, key=hops, reverse=True):
        pltpu.make_async_remote_copy(
            src_ref=seen.at[mine], dst_ref=seen.at[mine], send_sem=gsend.at[0],
            recv_sem=grecv.at[0],
            device_id={axis: along[axis][d] for axis, d in zip(AXES, offset)},
            device_id_type=MESH,
        ).start()
    wait_sends()
    others = seen.at[pl.ds(0, len(offsets))]
    pltpu.make_async_copy(others, others, grecv.at[0]).wait()
    terms = [seen[k] for k in range(len(offsets) + 1)]
    while len(terms) > 1:
        terms = [a + b for a, b in zip(terms[::2], terms[1::2])]
    value = terms[0]
    gram_ref[...] = value
    pltpu.make_async_copy(others, others, gsend.at[0]).wait()


def solve_kernel(filt, gram_ref, out_hbm, factor_hbm, out, factor_ref, out_sem, factor_sem):
    def entry(i, j):
        at = NORB * (i % SUB) + j
        return jnp.broadcast_to(gram_ref[i // SUB : i // SUB + 1, at : at + 1], (SUB, LX))

    row = lax.broadcasted_iota(jnp.int32, (SUB, LX), 0)
    lane = lax.broadcasted_iota(jnp.int32, (SUB, LX), 1)
    lower, inverse = {}, []
    for j in range(NORB):
        column = {i: entry(i, j) for i in range(j, NORB)}
        for k in range(j):
            for i in range(j, NORB):
                column[i] = column[i] - lower[i, k] * lower[j, k]
        root = jnp.sqrt(column[j])
        scale = F32(1) / root
        lower[j, j] = root
        for i in range(j + 1, NORB):
            lower[i, j] = column[i] * scale
        line = jnp.where(lane == j, F32(1), F32(0))
        for m in range(j):
            line = line - lower[j, m] * inverse[m]
        inverse.append(line * scale)

    def stack(lines):
        halves = []
        for half in range(GROUPS):
            rows = lines[half * SUB]
            for i in range(1, SUB):
                rows = jnp.where(row == i, lines[half * SUB + i], rows)
            halves.append(rows)
        return jnp.concatenate(halves, axis=0)

    def gather(entries):
        lines = []
        for i in range(NORB):
            line = jnp.zeros((SUB, LX), F32)
            for j in range(NORB):
                if (i, j) in entries:
                    line = jnp.where(lane == j, entries[i, j], line)
            lines.append(line)
        return stack(lines)

    high, low = split(stack(inverse)[:, :NORB])
    lhs = jnp.concatenate([high, high, low], axis=1)

    factor_ref[...] = gather({(j, i): value for (i, j), value in lower.items()})[:, :NORB]
    factor_copy = pltpu.make_async_copy(factor_ref, factor_hbm, factor_sem)

    def out_copy(c):
        part = pl.ds(c * STEP * LY, STEP * LY)
        return pltpu.make_async_copy(out.at[:, part], out_hbm.at[:, part], out_sem.at[c])

    for c in range(LZ // STEP):
        for z in range(c * STEP, (c + 1) * STEP):
            wide = jnp.concatenate(
                [
                    jnp.concatenate([filt[g, z, y] for g in range(GROUPS)], axis=0)
                    for y in range(LY)
                ],
                axis=1,
            )
            high, low = split(wide)
            solved = jnp.dot(
                lhs, jnp.concatenate([high, low, high], axis=0), preferred_element_type=F32
            )
            for g in range(GROUPS):
                for start in range(0, LY, SUB):
                    block = jnp.stack(
                        [
                            solved[g * SUB : (g + 1) * SUB, y * LX : (y + 1) * LX]
                            for y in range(start, start + SUB)
                        ]
                    )
                    out[pl.ds(g * SUB, SUB), pl.ds(z * LY + start, SUB), :] = jnp.swapaxes(
                        block, 0, 1
                    )
        out_copy(c).start(priority=c % 2)
        if c == 0:
            factor_copy.start()
    factor_copy.wait()
    for c in range(LZ // STEP):
        out_copy(c).wait()


def on_device(orbitals, potential):
    hbm = pl.BlockSpec(memory_space=pltpu.HBM)
    vmem = pl.BlockSpec(memory_space=pltpu.VMEM)
    dma = pltpu.SemaphoreType.DMA
    sizes = {axis: lax.axis_size(axis) for axis in AXES}
    filtered, gram = pl.pallas_call(
        filter_kernel,
        name="filter_and_gram",
        out_shape=[
            jax.ShapeDtypeStruct((GROUPS, LZ, LY, SUB, LX), F32),
            jax.ShapeDtypeStruct((2, LX), F32),
        ],
        in_specs=[hbm] * 3,
        out_specs=[vmem, vmem],
        scratch_shapes=[
            pltpu.VMEM((NORB, ROWS, LX), F32),
            *[pltpu.VMEM((GROUPS, LZ + 2 * HALO, LY + 2 * HALO, SUB, LX), F32)] * 3,
            *[pltpu.VMEM((GROUPS, LZ, SUB, LX), F32)] * 3,
            *[pltpu.VMEM((3, GROUPS, LZ, SUB, LX), F32)] * 2,
            pltpu.VMEM((LZ, LY, LX), F32),
            pltpu.VMEM((4 * LX, LX), BF16),
            pltpu.VMEM((NORB, LX), F32),
            pltpu.VMEM((sizes["gx"] * sizes["gy"] * sizes["gz"], 2, LX), F32),
            pltpu.SemaphoreType.REGULAR((4,)),
            dma((UNITS,)),
            dma((2,)),
            dma((3, UNITS, 2)),
            dma((3, UNITS, 2)),
            dma((3, UNITS, 2)),
            dma((3, UNITS, 2)),
            dma((3, GROUPS, 2)),
            dma((3, GROUPS, 2)),
            dma((1,)),
            dma((1,)),
        ],
        compiler_params=pltpu.CompilerParams(
            collective_id=0, has_side_effects=True, vmem_limit_bytes=40 * 2**20
        ),
        cost_estimate=pl.CostEstimate(
            flops=10**9, bytes_accessed=5 * 2**20, transcendentals=0
        ),
    )(*[
        pltpu.with_memory_space_constraint(value, pltpu.HBM)
        for value in (
            orbitals.reshape(NORB, ROWS, LX), potential, jnp.asarray(x_weights())
        )
    ])
    solved, factor = pl.pallas_call(
        solve_kernel,
        name="solve",
        out_shape=[
            jax.ShapeDtypeStruct((NORB, ROWS, LX), F32),
            jax.ShapeDtypeStruct((NORB, NORB), F32),
        ],
        in_specs=[vmem, vmem],
        out_specs=[hbm, hbm],
        scratch_shapes=[
            pltpu.VMEM((NORB, ROWS, LX), F32),
            pltpu.VMEM((NORB, NORB), F32),
            dma((LZ // STEP,)),
            dma(()),
        ],
        compiler_params=pltpu.CompilerParams(vmem_limit_bytes=24 * 2**20),
        cost_estimate=pl.CostEstimate(
            flops=10**8, bytes_accessed=4 * 2**20, transcendentals=0
        ),
    )(filtered, gram)
    return solved.reshape(NORB, LZ, LY, LX), factor


def solution(mesh):
    in_specs = (P(None, "gz", "gy", "gx"), P("gz", "gy", "gx"))
    out_specs = (P(None, "gz", "gy", "gx"), P())
    return jax.shard_map(
        on_device, mesh=mesh, in_specs=in_specs, out_specs=out_specs, check_vma=False
    )
```
